32 devices in a mesh: groups: 2 (over y), ctx: 4 (over z), head: 4 (over x, core).
Axes of the slice: x: 2, y: 2, z: 4, core: 2. Of those that a mesh axis runs over, the one named last changes fastest.
Arguments:
- q_block: bfloat16 [2048, 8192], P(('groups', 'ctx'), 'head'), parts along dimension 0, may hold values from -6 to 6
- kv_block: bfloat16 [2, 2048, 1024], P(None, ('groups', 'ctx'), 'head'), parts along dimension 1, may hold values from -6 to 6
- anchor_kv: bfloat16 [2, 1024, 1024], P(None, ('groups', 'ctx'), 'head'), parts along dimension 1, may hold values from -6 to 6
- cache_kv: bfloat16 [2, 32768, 1024], P(None, ('groups', 'ctx'), 'head'), parts along dimension 1, may hold values from -6 to 6
- cache_len: int32 [8], P(('groups', 'ctx')), parts along dimension 0, may hold values from 1 to 4096, 8192 in all
- query_q: bfloat16 [128, 8192], P(('groups', 'ctx'), 'head'), parts along dimension 0, may hold values from -6 to 6
- query_kv: bfloat16 [2, 128, 1024], P(None, ('groups', 'ctx'), 'head'), parts along dimension 1, may hold values from -6 to 6
- query_pos: int32 [128], P('groups'), parts along dimension 0, may hold values from 0 to 63, each once
Outputs:
- block_out: bfloat16 [2048, 8192], P(('groups', 'ctx'), 'head'), parts along dimension 0
- query_out: bfloat16 [128, 8192], P(('groups', 'ctx'), 'head'), parts along dimension 0
The draws below stay inside these ranges and needn't reach their ends.
There are 2 independent parts, one for each index of `groups`. The reference program is written for one: setup_inputs(seed, part) draws one part's arguments, and reference() takes and returns one part's arrays. A program takes and returns all parts, laid end to end along the dimension named above; each array names one. Nothing has to cross between parts.
All inputs are finite; a program needn't handle non-finite values. No bound on the sum of `cache_len` on one device may be relied on, other than what follows from the above.
Results may differ from the reference program's by a relative error of at most 0.0034.
Values may be sent and summed in bfloat16 or wider, within the bound.
A program may use at most 128 MiB of HBM per device.

```python
import math
import jax
import jax.numpy as jnp
import numpy as np
from jax import lax

HQ = 64
KVH = 8
HD = 128
CACHE_DEV = 4096
BLK = 256
ANCHOR = 512
QTOK = 64
HOSTS = 4


def pair_rows(key, salt, row_total, span):
    own_key = jax.random.fold_in(key, salt)
    noise = jax.random.normal(jax.random.fold_in(own_key, 1), (2, row_total, KVH * HD), jnp.float32)
    centers = jax.random.normal(jax.random.fold_in(own_key, 2), (2, row_total // span, KVH * HD), jnp.float32)
    centers = jnp.repeat(centers, span, axis=1)
    key_part = noise[0] + 0.8 * centers[0]
    value_part = 0.6 * noise[1] + centers[1]
    return jnp.clip(jnp.stack([key_part, value_part]), -6.0, 6.0).astype(jnp.bfloat16)


def query_rows(key, salt, row_total):
    base = jax.random.normal(jax.random.fold_in(key, salt), (row_total, HQ * HD), jnp.float32)
    base = jnp.clip(base, -6.0, 6.0)
    return base.astype(jnp.bfloat16)


def draw_q_block(key, part):
    return query_rows(key, 11, HOSTS * BLK)


def draw_anchor_kv(key, part):
    return pair_rows(key, 12, ANCHOR, 2)


def draw_kv_block(key, part):
    return pair_rows(key, 13, HOSTS * BLK, BLK)


def draw_cache_kv(key, part):
    return pair_rows(key, 14, HOSTS * CACHE_DEV, CACHE_DEV)


def draw_query_q(key, part):
    return query_rows(key, 15, QTOK)


def draw_query_kv(key, part):
    return pair_rows(key, 16, QTOK, 2)


def length_profile(count, total, most, slope):
    weights = [(1 << 20) // math.isqrt(rank ** slope) + 1 for rank in range(2, count + 1)]
    spare, holding = total - most - (count - 1), [1] * (count - 1)
    while spare > 0:
        free = [i for i in range(count - 1) if holding[i] < most]
        mass, budget = sum([weights[i] for i in free]), spare
        for i in free:
            extra = min(most - holding[i], max(1, budget * weights[i] // mass), spare)
            holding[i] = holding[i] + extra
            spare = spare - extra
    return np.array([most] + holding)


def ragged(key, number_of, total, most, slope):
    if number_of == 2:
        one = jax.random.randint(key, (), max(1, total - most), min(most, total - 1) + 1)
        return jnp.stack([one, total - one])
    tallies = jnp.asarray(length_profile(number_of, total, most, slope), jnp.int32)
    twos = (number_of - 1) // 2
    donor, taker = tallies[1:1 + 2 * twos:2], tallies[2:2 + 2 * twos:2]
    room = jnp.minimum(donor - 1, most - taker)
    moved = jax.random.randint(jax.random.fold_in(key, 1), (twos,), 0, 1 << 20) % (room + 1)
    tallies = tallies.at[1:1 + 2 * twos:2].set(donor - moved).at[2:2 + 2 * twos:2].set(taker + moved)
    return tallies[jax.random.permutation(jax.random.fold_in(key, 2), number_of)]


def setup_inputs(seed: int = 0, part: int = 0) -> dict:
    key_of = jax.random.split(jax.random.key(seed), 9)
    part_splits = jax.random.split(jax.random.fold_in(key_of[8], part), 9)
    return {
        "q_block": draw_q_block(jax.random.fold_in(jax.random.fold_in(key_of[8], part), 71), part),
        "kv_block": draw_kv_block(jax.random.fold_in(jax.random.fold_in(key_of[8], part), 71), part),
        "anchor_kv": draw_anchor_kv(jax.random.fold_in(jax.random.fold_in(key_of[8], part), 71), part),
        "cache_kv": draw_cache_kv(jax.random.fold_in(jax.random.fold_in(key_of[8], part), 71), part),
        "cache_len": ragged(part_splits[4], HOSTS, HOSTS * CACHE_DEV // 2, CACHE_DEV, 2).astype(jnp.int32),
        "query_q": draw_query_q(jax.random.fold_in(jax.random.fold_in(key_of[8], part), 71), part),
        "query_kv": draw_query_kv(jax.random.fold_in(jax.random.fold_in(key_of[8], part), 71), part),
        "query_pos": jax.random.permutation(part_splits[7], QTOK).astype(jnp.int32),
    }


masked_score = -1e+30

def widen(per_head):
    return jnp.repeat(per_head, HD, axis=-1)

def partial_attention(queries, key_rows, value_rows, visible):
    row_count = queries.shape[0]
    key_count = key_rows.shape[0]
    kv_heads = key_rows.shape[1] // HD
    query_heads = queries.shape[1] // HD
    group_size = query_heads // kv_heads
    grouped = queries.astype(jnp.float32).reshape(row_count, kv_heads, group_size, HD)
    key_heads = key_rows.astype(jnp.float32).reshape(key_count, kv_heads, HD)
    scores = jnp.einsum('rkgd,skd->rkgs', grouped, key_heads, precision=lax.Precision.HIGHEST) * (1.0 / jnp.sqrt(jnp.float32(HD)))
    scores = jnp.where(visible[:, None, None, :], scores, masked_score)
    peak_score = lax.optimization_barrier(jnp.max(scores, axis=-1))
    weights = jnp.exp(scores - peak_score[..., None])
    totals = lax.optimization_barrier(jnp.sum(weights, axis=-1))
    rounded = weights.astype(jnp.bfloat16).astype(jnp.float32)
    value_heads = value_rows.astype(jnp.float32).reshape(key_count, kv_heads, HD)
    output = jnp.einsum('rkgs,skd->rkgd', rounded, value_heads, precision=lax.Precision.HIGHEST)
    return (peak_score.reshape(row_count, query_heads), totals.reshape(row_count, query_heads), output.reshape(row_count, query_heads * HD))

def reference(q_block, kv_block, anchor_kv, cache_kv, cache_len, query_q, query_kv, query_pos):
    causal = jnp.arange(BLK)[None, :] <= jnp.arange(BLK)[:, None]
    block_visible = jnp.concatenate([jnp.ones((BLK, ANCHOR), bool), causal], axis=1)

    def encode(host_index):
        block_rows = lax.dynamic_slice_in_dim(q_block, host_index * BLK, BLK, 0)
        block_pair = lax.dynamic_slice_in_dim(kv_block, host_index * BLK, BLK, 1)
        parts = partial_attention(block_rows, jnp.concatenate([anchor_kv[0], block_pair[0]], axis=0), jnp.concatenate([anchor_kv[1], block_pair[1]], axis=0), block_visible)
        return (parts[2] / widen(parts[1])).astype(jnp.bfloat16)
    block_out = lax.map(encode, jnp.arange(HOSTS, dtype=jnp.int32)).reshape(HOSTS * BLK, HQ * HD)

    def context(host_index):
        cache_pair = lax.dynamic_slice_in_dim(cache_kv, host_index * CACHE_DEV, CACHE_DEV, 1)
        block_pair = lax.dynamic_slice_in_dim(kv_block, host_index * BLK, BLK, 1)
        in_cache = jnp.arange(CACHE_DEV, dtype=jnp.int32) < cache_len[host_index]
        visible = jnp.concatenate([jnp.broadcast_to(in_cache[None, :], (QTOK, CACHE_DEV)), jnp.ones((QTOK, BLK), bool)], axis=1)
        return partial_attention(query_q, jnp.concatenate([cache_pair[0], block_pair[0]], axis=0), jnp.concatenate([cache_pair[1], block_pair[1]], axis=0), visible)
    peaks, totals, outputs = lax.map(context, jnp.arange(HOSTS, dtype=jnp.int32))
    local_visible = jnp.concatenate([jnp.ones((QTOK, ANCHOR), bool), query_pos[None, :] <= query_pos[:, None]], axis=1)
    local_peak, local_totals, local_output = partial_attention(query_q, jnp.concatenate([anchor_kv[0], query_kv[0]], axis=0), jnp.concatenate([anchor_kv[1], query_kv[1]], axis=0), local_visible)
    top_score = jnp.maximum(lax.optimization_barrier(jnp.max(peaks, axis=0)), local_peak)
    factors = jnp.exp(peaks - top_score[None])
    local_factor = jnp.exp(local_peak - top_score)
    merged_totals = lax.optimization_barrier(jnp.sum(totals * factors, axis=0)) + local_totals * local_factor
    merged_output = lax.optimization_barrier(jnp.sum(outputs * widen(factors), axis=0)) + local_output * widen(local_factor)
    return (block_out, (merged_output / widen(merged_totals)).astype(jnp.bfloat16))
```

```python
import functools
import math

import jax
import jax.numpy as jnp
from jax import lax
from jax.experimental import pallas as pl
from jax.experimental.pallas import tpu as pltpu
from jax.sharding import PartitionSpec as P

HD = 128
NEG = -1e30
SCALE2 = math.log2(math.e) / math.sqrt(HD)
CHUNK = 512
MESH = pl.DeviceIdType.MESH


def scores(queries, keys):
    dims = (((1,), (1,)), ((), ()))
    return lax.dot_general(queries, keys, dims, preferred_element_type=jnp.float32) * SCALE2


def with_ones(values):
    return jnp.concatenate([values, jnp.ones_like(values)], axis=1)


def weighted(weights, values):
    return jnp.dot(weights.astype(jnp.bfloat16), values, preferred_element_type=jnp.float32)


def kernel(
    n, own,
    pos_ref, len_ref, q_hbm, kv_hbm, anchor_hbm, cache_hbm, qq_hbm, qkv_hbm,
    out_ref, qout_ref,
    q_buf, kv_buf, cache_buf, qkv_buf, anchors, queries,
    qg, kx, vx, xbias, s_buf, m_run, acc, kb, vb, causal,
    send_o, send_st, recv_o, recv_st,
    in_sem, q_send, q_recv, a_send, a_recv, o_send, o_recv, st_send, st_recv,
):
    me = lax.axis_index("ctx")
    peers = [lax.rem(me + k, n) for k in range(1, n)]
    rows = qq_hbm.shape[0]
    block = q_buf.shape[0]
    columns = q_buf.shape[1]
    kv_heads = kv_buf.shape[2] // HD
    group = columns // HD // kv_heads
    share = anchor_hbm.shape[1]
    cache_count = cache_buf.shape[1]
    total = n * rows
    extra = kx.shape[1]
    tile = s_buf.shape[0]
    tile_heads = tile // total
    half = group * HD

    loads = [
        pltpu.make_async_copy(qq_hbm, queries.at[pl.ds(pl.multiple_of(me * rows, rows), rows)], in_sem.at[0]),
        pltpu.make_async_copy(anchor_hbm, anchors.at[me], in_sem.at[1]),
        pltpu.make_async_copy(kv_hbm, kv_buf, in_sem.at[2]),
        pltpu.make_async_copy(qkv_hbm, qkv_buf, in_sem.at[3]),
        pltpu.make_async_copy(cache_hbm, cache_buf, in_sem.at[4]),
        pltpu.make_async_copy(q_hbm, q_buf, in_sem.at[5]),
    ]
    for load in loads:
        load.start()

    barrier = pltpu.get_barrier_semaphore()
    for peer in peers:
        pl.semaphore_signal(barrier, inc=1, device_id={"ctx": peer}, device_id_type=MESH)
    pl.semaphore_wait(barrier, n - 1)

    def own_rows(ref, who):
        return ref.at[pl.ds(pl.multiple_of(who * rows, rows), rows)]

    def query_copy(slot, peer):
        return pltpu.make_async_remote_copy(
            src_ref=qq_hbm, dst_ref=own_rows(queries, slot), send_sem=q_send.at[peer],
            recv_sem=q_recv.at[slot], device_id={"ctx": peer}, device_id_type=MESH)

    def anchor_copy(slot, peer):
        return pltpu.make_async_remote_copy(
            src_ref=anchor_hbm, dst_ref=anchors.at[slot], send_sem=a_send.at[peer],
            recv_sem=a_recv.at[slot], device_id={"ctx": peer}, device_id_type=MESH)

    def output_copy(g, slot, peer):
        cols = pl.ds(g * half, half)
        return pltpu.make_async_remote_copy(
            src_ref=send_o.at[pl.ds(pl.multiple_of(peer * rows, rows), rows), cols],
            dst_ref=recv_o.at[slot, :, cols], send_sem=o_send.at[g, peer],
            recv_sem=o_recv.at[g, slot], device_id={"ctx": peer}, device_id_type=MESH)

    def stats_copy(slot, peer):
        return pltpu.make_async_remote_copy(
            src_ref=send_st.at[:, pl.ds(pl.multiple_of(peer * rows, rows), rows)],
            dst_ref=recv_st.at[slot], send_sem=st_send.at[peer],
            recv_sem=st_recv.at[slot], device_id={"ctx": peer}, device_id_type=MESH)

    for peer in peers:
        query_copy(me, peer).start()
    for peer in peers:
        anchor_copy(me, peer).start()

    row = lax.broadcasted_iota(jnp.int32, (total, HD), 0)
    lane = lax.broadcasted_iota(jnp.int32, (total, HD), 1)
    row_pos = jnp.zeros((total, HD), jnp.int32)
    for i in range(n * own):
        row_pos = jnp.where(row == (i // own) * rows + i % own, pos_ref[i], row_pos)
    key_pos = jnp.full((total, HD), 1 << 30, jnp.int32)
    for j in range(own):
        key_pos = jnp.where(lane == j, pos_ref[me * own + j], key_pos)
    xbias[...] = jnp.where(key_pos <= row_pos, 0.0, NEG)
    send_st[...] = jnp.zeros_like(send_st)
    first = lax.broadcasted_iota(jnp.int32, (block, block), 0)
    second = lax.broadcasted_iota(jnp.int32, (block, block), 1)
    causal[...] = jnp.where(second <= first, 0.0, NEG)

    for load in loads:
        load.wait()
    for g in range(kv_heads):
        cols = slice(g * HD, (g + 1) * HD)
        for half_index, target in ((0, kx), (1, vx)):
            target[g, 0:block] = kv_buf[half_index, :, cols]
            target[g, pl.ds(block, share)] = anchors[me, half_index, :, cols]
            target[g, pl.ds(block + share, rows)] = qkv_buf[half_index, :, cols]
            rest = extra - block - share - rows
            if rest:
                target[g, pl.ds(block + share + rows, rest)] = jnp.zeros((rest, HD), jnp.bfloat16)

    for peer in peers:
        query_copy(peer, peer).wait_recv()

    length = len_ref[0]
    chunk_lane = lax.broadcasted_iota(jnp.int32, (1, CHUNK), 1)

    def fold(block_scores):
        parts = [block_scores[:, k:k + HD] for k in range(0, block_scores.shape[1], HD)]
        return functools.reduce(jnp.maximum, parts)

    for g in range(kv_heads):
        cols = slice(g * HD, (g + 1) * HD)

        def one_tile(t, carry):
            for j in range(tile_heads):
                head = g * group + t * tile_heads + j
                qg[j * total:(j + 1) * total] = queries[:, pl.ds(pl.multiple_of(head * HD, HD), HD)]
            near = scores(qg[...], kx[g])
            tail = jnp.concatenate([xbias[...]] * tile_heads, axis=0)
            edge = block + share
            near_parts = [near[:, :edge], near[:, edge:edge + HD] + tail]
            if extra > edge + HD:
                near_parts.append(jnp.full((tile, extra - edge - HD), NEG, jnp.float32))
            near = jnp.concatenate(near_parts, axis=1)
            s_buf[:, cache_count:] = near
            m_run[...] = fold(near)

            def cached_scores(i, carry):
                at = pl.multiple_of(i * CHUNK, CHUNK)
                bias = jnp.where(chunk_lane + at < length, 0.0, NEG)
                part = scores(qg[...], cache_buf[0, pl.ds(at, CHUNK), cols]) + bias
                s_buf[:, pl.ds(at, CHUNK)] = part
                m_run[...] = jnp.maximum(m_run[...], fold(part))
                return carry

            lax.fori_loop(0, cache_count // CHUNK, cached_scores, 0)
            peak = jnp.max(m_run[...], axis=1, keepdims=True)
            m_run[...] = jnp.broadcast_to(peak, m_run.shape)
            weights = jnp.exp2(s_buf[:, cache_count:] - m_run[:, 0:1])
            acc[...] = weighted(weights, with_ones(vx[g]))

            def cached_values(i, carry):
                at = pl.multiple_of(i * CHUNK, CHUNK)
                weights = jnp.exp2(s_buf[:, pl.ds(at, CHUNK)] - m_run[:, 0:1])
                acc[...] += weighted(weights, with_ones(cache_buf[1, pl.ds(at, CHUNK), cols]))
                return carry

            lax.fori_loop(0, cache_count // CHUNK, cached_values, 0)
            for j in range(tile_heads):
                head = g * group + t * tile_heads + j
                span = slice(j * total, (j + 1) * total)
                send_o[:, pl.ds(pl.multiple_of(head * HD, HD), HD)] = acc[span, :HD].astype(jnp.bfloat16)
                send_st[0] = jnp.where(lane == head, m_run[span], send_st[0])
                send_st[1] = jnp.where(lane == head, acc[span, HD:], send_st[1])
            return carry

        if group == tile_heads:
            one_tile(0, 0)
        else:
            lax.fori_loop(0, group // tile_heads, one_tile, 0)
        for peer in peers:
            output_copy(g, me, peer).start()
    for peer in peers:
        stats_copy(me, peer).start()

    for peer in peers:
        anchor_copy(peer, peer).wait_recv()
    for g in range(kv_heads):
        cols = slice(g * HD, (g + 1) * HD)
        for c in range(n):
            kb[g, c * share:(c + 1) * share] = anchors[c, 0, :, cols]
            vb[g, c * share:(c + 1) * share] = with_ones(anchors[c, 1, :, cols])
        kb[g, pl.ds(n * share, block)] = kv_buf[0, :, cols]
        vb[g, pl.ds(n * share, block)] = with_ones(kv_buf[1, :, cols])

        def one_head(j, carry):
            span = pl.ds(pl.multiple_of((g * group + j) * HD, HD), HD)
            part = scores(q_buf[:, span], kb[g])
            part = jnp.concatenate([part[:, :n * share], part[:, n * share:] + causal[...]], axis=1)
            weights = jnp.exp2(part - jnp.max(part, axis=1, keepdims=True))
            result = weighted(weights, vb[g])
            out_ref[:, span] = (result[:, :HD] / result[:, HD:]).astype(jnp.bfloat16)
            return carry

        lax.fori_loop(0, group, one_head, 0, unroll=2)

    for peer in peers:
        stats_copy(peer, peer).wait_recv()
        for g in range(kv_heads):
            output_copy(g, peer, peer).wait_recv()
    mine = pl.ds(pl.multiple_of(me * rows, rows), rows)
    recv_st[me] = send_st[:, mine]
    recv_o[me] = send_o[mine]
    top = functools.reduce(jnp.maximum, [recv_st[c, 0] for c in range(n)])
    factors = [jnp.exp2(recv_st[c, 0] - top) for c in range(n)]
    whole = sum(factors[c] * recv_st[c, 1] for c in range(n))
    heads = columns // HD
    for h in range(heads):
        span = slice(h * HD, (h + 1) * HD)
        merged = sum(
            recv_o[c, :, span].astype(jnp.float32) * factors[c][:, h:h + 1] for c in range(n)
        )
        qout_ref[:, span] = (merged / whole[:, h:h + 1]).astype(jnp.bfloat16)

    for peer in peers:
        query_copy(me, peer).wait_send()
        anchor_copy(me, peer).wait_send()
        stats_copy(me, peer).wait_send()
        for g in range(kv_heads):
            output_copy(g, me, peer).wait_send()


def local(n, q_block, kv_block, anchor_kv, cache_kv, cache_len, query_q, query_kv, query_pos):
    own = query_q.shape[0]
    rows = -(-own // 16) * 16
    if rows != own:
        query_q = jnp.pad(query_q, ((0, rows - own), (0, 0)))
        query_kv = jnp.pad(query_kv, ((0, 0), (0, rows - own), (0, 0)))
    block, columns = q_block.shape
    kv_columns = kv_block.shape[2]
    kv_heads = kv_columns // HD
    group = columns // kv_columns
    share = anchor_kv.shape[1]
    cache_count = cache_kv.shape[1]
    total = n * rows
    tile = total * max(1, min(group, 512 // total))
    extra = -(-(block + share + HD) // HD) * HD
    keys = n * share + block
    bf16, f32 = jnp.bfloat16, jnp.float32
    vmem = pltpu.VMEM
    dma = pltpu.SemaphoreType.DMA
    hbm = pl.BlockSpec(memory_space=pl.ANY)
    smem = pl.BlockSpec(memory_space=pltpu.SMEM)
    block_out, query_out = pl.pallas_call(
        functools.partial(kernel, n, own),
        out_shape=(
            jax.ShapeDtypeStruct((block, columns), bf16),
            jax.ShapeDtypeStruct((rows, columns), bf16),
        ),
        in_specs=[smem, smem] + [hbm] * 6,
        out_specs=(pl.BlockSpec(memory_space=vmem), pl.BlockSpec(memory_space=vmem)),
        scratch_shapes=[
            vmem((block, columns), bf16),
            vmem((2, block, kv_columns), bf16),
            vmem((2, cache_count, kv_columns), bf16),
            vmem((2, rows, kv_columns), bf16),
            vmem((n, 2, share, kv_columns), bf16),
            vmem((total, columns), bf16),
            vmem((tile, HD), bf16),
            vmem((kv_heads, extra, HD), bf16),
            vmem((kv_heads, extra, HD), bf16),
            vmem((total, HD), f32),
            vmem((tile, cache_count + extra), f32),
            vmem((tile, HD), f32),
            vmem((tile, 2 * HD), f32),
            vmem((kv_heads, keys, HD), bf16),
            vmem((kv_heads, keys, 2 * HD), bf16),
            vmem((block, block), f32),
            vmem((total, columns), bf16),
            vmem((2, total, HD), f32),
            vmem((n, rows, columns), bf16),
            vmem((n, 2, rows, HD), f32),
            dma((6,)),
            dma((n,)), dma((n,)), dma((n,)), dma((n,)),
            dma((kv_heads, n)), dma((kv_heads, n)),
            dma((n,)), dma((n,)),
        ],
        compiler_params=pltpu.CompilerParams(
            collective_id=0, has_side_effects=True, vmem_limit_bytes=56 * 1024 * 1024
        ),
    )(query_pos, cache_len, q_block, kv_block, anchor_kv, cache_kv, query_q, query_kv)
    return block_out, query_out[:own]


def solution(mesh):
    in_specs = (
        P(("groups", "ctx"), "head"),
        P(None, ("groups", "ctx"), "head"),
        P(None, ("groups", "ctx"), "head"),
        P(None, ("groups", "ctx"), "head"),
        P(("groups", "ctx")),
        P(("groups", "ctx"), "head"),
        P(None, ("groups", "ctx"), "head"),
        P("groups"),
    )
    out_specs = (P(("groups", "ctx"), "head"), P(("groups", "ctx"), "head"))
    return jax.shard_map(
        functools.partial(local, mesh.shape["ctx"]),
        mesh=mesh, in_specs=in_specs, out_specs=out_specs, check_vma=False)
```

```python
import functools
import math

import jax
import jax.numpy as jnp
from jax import lax
from jax.experimental import pallas as pl
from jax.experimental.pallas import tpu as pltpu
from jax.sharding import PartitionSpec as P

HD = 128
NEG = -1e30
SCALE2 = math.log2(math.e) / math.sqrt(HD)
CHUNK = 1024
TRIM = 256
MESH = pl.DeviceIdType.MESH


def scores(queries, keys):
    dims = (((1,), (1,)), ((), ()))
    return lax.dot_general(queries, keys, dims, preferred_element_type=jnp.float32) * SCALE2


def with_ones(values):
    return jnp.concatenate([values, jnp.ones_like(values)], axis=1)


def weighted(weights, values):
    return jnp.dot(weights.astype(jnp.bfloat16), values, preferred_element_type=jnp.float32)


def kernel(
    n, own,
    pos_ref, len_hbm, q_hbm, kv_hbm, anchor_hbm, cache_hbm, qq_hbm, qkv_hbm,
    out_hbm, qout_ref,
    len_ref, q_buf, kv_buf, cache_buf, qkv_buf, anchors, queries,
    qg, kx, vx, ones, xbias, s_buf, m_run, acc, kb, vb, causal, m_blk, o_blk, out_buf,
    send_o, send_st, recv_o, recv_st,
    in_sem, out_sem, q_send, q_recv, a_send, a_recv, o_send, o_recv, st_send, st_recv,
):
    me = lax.axis_index("ctx")
    peers = [lax.rem(me + k, n) for k in range(1, n)]
    rows = qq_hbm.shape[0]
    block = q_buf.shape[0]
    columns = q_buf.shape[1]
    kv_heads = kv_buf.shape[2] // HD
    group = columns // HD // kv_heads
    share = anchor_hbm.shape[1]
    cache_count = cache_buf.shape[1]
    total = n * rows
    extra = kx.shape[1]
    tile = s_buf.shape[0]
    tile_heads = tile // total
    half = group * HD
    near_keys = block + share

    def rows_of(who):
        return pl.ds(pl.multiple_of(who * rows, rows), rows)

    def half_of(g):
        return pl.ds(g * half, half)

    loads = [
        pltpu.make_async_copy(qq_hbm, queries.at[rows_of(me)], in_sem.at[0]),
        pltpu.make_async_copy(anchor_hbm, anchors.at[me], in_sem.at[1]),
        pltpu.make_async_copy(kv_hbm, kv_buf, in_sem.at[2]),
        pltpu.make_async_copy(qkv_hbm, qkv_buf, in_sem.at[3]),
        pltpu.make_async_copy(q_hbm, q_buf, in_sem.at[4]),
        pltpu.make_async_copy(len_hbm, len_ref, in_sem.at[5]),
    ]
    cache_load = pltpu.make_async_copy(cache_hbm, cache_buf, in_sem.at[6])
    for load in loads:
        load.start()
    cache_load.start()

    barrier = pltpu.get_barrier_semaphore()
    for peer in peers:
        pl.semaphore_signal(barrier, inc=1, device_id={"ctx": peer}, device_id_type=MESH)
    pl.semaphore_wait(barrier, n - 1)

    def query_copy(g, slot, peer):
        return pltpu.make_async_remote_copy(
            src_ref=qq_hbm.at[:, half_of(g)], dst_ref=queries.at[rows_of(slot), half_of(g)],
            send_sem=q_send.at[g, peer], recv_sem=q_recv.at[g, slot],
            device_id={"ctx": peer}, device_id_type=MESH)

    def anchor_copy(slot, peer):
        return pltpu.make_async_remote_copy(
            src_ref=anchor_hbm, dst_ref=anchors.at[slot], send_sem=a_send.at[peer],
            recv_sem=a_recv.at[slot], device_id={"ctx": peer}, device_id_type=MESH)

    def output_copy(g, slot, peer):
        return pltpu.make_async_remote_copy(
            src_ref=send_o.at[rows_of(peer), half_of(g)],
            dst_ref=recv_o.at[slot, :, half_of(g)], send_sem=o_send.at[g, peer],
            recv_sem=o_recv.at[g, slot], device_id={"ctx": peer}, device_id_type=MESH)

    def stats_copy(slot, peer):
        return pltpu.make_async_remote_copy(
            src_ref=send_st.at[:, rows_of(peer)],
            dst_ref=recv_st.at[slot], send_sem=st_send.at[peer],
            recv_sem=st_recv.at[slot], device_id={"ctx": peer}, device_id_type=MESH)

    for g in range(kv_heads):
        for peer in peers:
            query_copy(g, me, peer).start()

    row = lax.broadcasted_iota(jnp.int32, (total, HD), 0)
    lane = lax.broadcasted_iota(jnp.int32, (total, HD), 1)
    row_pos = jnp.zeros((total, HD), jnp.int32)
    for i in range(n * own):
        row_pos = jnp.where(row == (i // own) * rows + i % own, pos_ref[i], row_pos)
    key_pos = jnp.full((total, HD), 1 << 30, jnp.int32)
    for j in range(own):
        key_pos = jnp.where(lane == j, pos_ref[me * own + j], key_pos)
    xbias[...] = jnp.where(key_pos <= row_pos, 0.0, NEG)
    send_st[...] = jnp.zeros_like(send_st)
    first = lax.broadcasted_iota(jnp.int32, (block, block), 0)
    second = lax.broadcasted_iota(jnp.int32, (block, block), 1)
    causal[...] = jnp.where(second <= first, 0.0, NEG)

    for load in loads:
        load.wait()
    for g in range(kv_heads):
        cols = slice(g * HD, (g + 1) * HD)
        for index, target in ((0, kx), (1, vx)):
            target[g, 0:block] = kv_buf[index, :, cols]
            target[g, pl.ds(block, share)] = anchors[me, index, :, cols]
            target[g, pl.ds(near_keys, rows)] = qkv_buf[index, :, cols]
            rest = extra - near_keys - rows
            if rest:
                target[g, pl.ds(near_keys + rows, rest)] = jnp.zeros((rest, HD), jnp.bfloat16)

    def fold(block_scores):
        parts = [block_scores[:, k:k + HD] for k in range(0, block_scores.shape[1], HD)]
        return functools.reduce(jnp.maximum, parts)

    def less(block_scores, peak):
        parts = [block_scores[:, k:k + HD] - peak for k in range(0, block_scores.shape[1], HD)]
        return jnp.concatenate(parts, axis=1)

    for g in range(kv_heads):

        def near_head(j, carry):
            head = g * group + j
            span = pl.ds(pl.multiple_of(head * HD, HD), HD)
            part = scores(q_buf[:, span], kx[g, pl.ds(0, near_keys)])
            part = jnp.concatenate([part[:, :block] + causal[...], part[:, block:]], axis=1)
            peak = jnp.max(part, axis=1, keepdims=True)
            m_blk[head] = jnp.broadcast_to(peak, (block, HD))
            o_blk[head] = weighted(jnp.exp2(part - peak), with_ones(vx[g, pl.ds(0, near_keys)]))
            return carry

        lax.fori_loop(0, group, near_head, 0, unroll=4)

    for peer in peers:
        anchor_copy(me, peer).start()

    length = len_ref[0]
    cache_load.wait()
    spare = kv_buf[0, 0:16, :][0:1]
    wide = cache_buf.shape[2]

    def trim(i, carry):
        at = pl.multiple_of(i * TRIM, TRIM)
        slot = lax.broadcasted_iota(jnp.int32, (TRIM, wide), 0) + at
        visible = jnp.where(slot < length, 1.0, 0.0).astype(jnp.bfloat16)
        keys = cache_buf[0, pl.ds(at, TRIM)]
        cache_buf[0, pl.ds(at, TRIM)] = keys * visible + spare * (1.0 - visible)
        cache_buf[1, pl.ds(at, TRIM)] = cache_buf[1, pl.ds(at, TRIM)] * visible
        ones[pl.ds(at, TRIM)] = visible[:, :HD]
        return carry

    lax.fori_loop(0, cache_count // TRIM, trim, 0)

    for g in range(kv_heads):
        cols = slice(g * HD, (g + 1) * HD)
        for peer in peers:
            query_copy(g, peer, peer).wait_recv()

        def one_tile(t, carry):
            for j in range(tile_heads):
                head = g * group + t * tile_heads + j
                qg[j * total:(j + 1) * total] = queries[:, pl.ds(pl.multiple_of(head * HD, HD), HD)]
            near = scores(qg[...], kx[g])
            tail = jnp.concatenate([xbias[...]] * tile_heads, axis=0)
            near_parts = [near[:, :near_keys], near[:, near_keys:near_keys + HD] + tail]
            if extra > near_keys + HD:
                near_parts.append(jnp.full((tile, extra - near_keys - HD), NEG, jnp.float32))
            near = jnp.concatenate(near_parts, axis=1)
            s_buf[:, cache_count:] = near
            m_run[...] = fold(near)

            def cached_scores(i, carry):
                at = pl.multiple_of(i * CHUNK, CHUNK)
                part = scores(qg[...], cache_buf[0, pl.ds(at, CHUNK), cols])
                s_buf[:, pl.ds(at, CHUNK)] = part
                m_run[...] = jnp.maximum(m_run[...], fold(part))
                return carry

            lax.fori_loop(0, cache_count // CHUNK, cached_scores, 0)
            peak = jnp.max(m_run[...], axis=1, keepdims=True)
            m_run[...] = jnp.broadcast_to(peak, m_run.shape)
            weights = jnp.exp2(less(s_buf[:, cache_count:], m_run[...]))
            acc[...] = weighted(weights, with_ones(vx[g]))

            def cached_values(i, carry):
                at = pl.multiple_of(i * CHUNK, CHUNK)
                weights = jnp.exp2(less(s_buf[:, pl.ds(at, CHUNK)], m_run[...]))
                values = jnp.concatenate(
                    [cache_buf[1, pl.ds(at, CHUNK), cols], ones[pl.ds(at, CHUNK)]], axis=1)
                acc[...] += weighted(weights, values)
                return carry

            lax.fori_loop(0, cache_count // CHUNK, cached_values, 0)
            for j in range(tile_heads):
                head = g * group + t * tile_heads + j
                span = slice(j * total, (j + 1) * total)
                send_o[:, pl.ds(pl.multiple_of(head * HD, HD), HD)] = acc[span, :HD].astype(jnp.bfloat16)
                send_st[0] = jnp.where(lane == head, m_run[span], send_st[0])
                send_st[1] = jnp.where(lane == head, acc[span, HD:], send_st[1])
            return carry

        if group == tile_heads:
            one_tile(0, 0)
        else:
            lax.fori_loop(0, group // tile_heads, one_tile, 0)
        for peer in peers:
            output_copy(g, me, peer).start()
    for peer in peers:
        stats_copy(me, peer).start()

    for peer in peers:
        anchor_copy(peer, peer).wait_recv()
    for g in range(kv_heads):
        cols = slice(g * HD, (g + 1) * HD)
        for k, peer in enumerate(peers):
            kb[g, k * share:(k + 1) * share] = anchors[peer, 0, :, cols]
            vb[g, k * share:(k + 1) * share] = with_ones(anchors[peer, 1, :, cols])

        def far_head(j, carry):
            head = g * group + j
            span = pl.ds(pl.multiple_of(head * HD, HD), HD)
            part = scores(q_buf[:, span], kb[g])
            before = m_blk[head]
            peak = jnp.maximum(before, jnp.max(part, axis=1, keepdims=True))
            result = weighted(jnp.exp2(part - peak[:, 0:1] if part.shape[1] % HD else less(part, peak)), vb[g])
            factor = jnp.exp2(before - peak)
            top = result[:, :HD] + o_blk[head, :, :HD] * factor
            below = result[:, HD:] + o_blk[head, :, HD:] * factor
            out_buf[:, span] = (top / below).astype(jnp.bfloat16)
            return carry

        lax.fori_loop(0, group, far_head, 0, unroll=4)
        pltpu.make_async_copy(out_buf.at[:, half_of(g)], out_hbm.at[:, half_of(g)], out_sem.at[g]).start()

    for peer in peers:
        stats_copy(peer, peer).wait_recv()
        for g in range(kv_heads):
            output_copy(g, peer, peer).wait_recv()
    mine = rows_of(me)
    recv_st[me] = send_st[:, mine]
    recv_o[me] = send_o[mine]
    top = functools.reduce(jnp.maximum, [recv_st[c, 0] for c in range(n)])
    factors = [jnp.exp2(recv_st[c, 0] - top) for c in range(n)]
    whole = sum(factors[c] * recv_st[c, 1] for c in range(n))
    heads = columns // HD
    for h in range(heads):
        span = slice(h * HD, (h + 1) * HD)
        merged = sum(
            recv_o[c, :, span].astype(jnp.float32) * factors[c][:, h:h + 1] for c in range(n)
        )
        qout_ref[:, span] = (merged / whole[:, h:h + 1]).astype(jnp.bfloat16)

    for g in range(kv_heads):
        pltpu.make_async_copy(out_buf.at[:, half_of(g)], out_hbm.at[:, half_of(g)], out_sem.at[g]).wait()
    for peer in peers:
        anchor_copy(me, peer).wait_send()
        stats_copy(me, peer).wait_send()
        for g in range(kv_heads):
            query_copy(g, me, peer).wait_send()
            output_copy(g, me, peer).wait_send()


def hand_on(block_in, query_in, block_out, query_out, sems):
    copies = [
        pltpu.make_async_copy(block_in, block_out, sems.at[0]),
        pltpu.make_async_copy(query_in, query_out, sems.at[1]),
    ]
    for copy in copies:
        copy.start()
    for copy in copies:
        copy.wait()


def local(n, q_block, kv_block, anchor_kv, cache_kv, cache_len, query_q, query_kv, query_pos):
    own = query_q.shape[0]
    rows = -(-own // 16) * 16
    if rows != own:
        query_q = jnp.pad(query_q, ((0, rows - own), (0, 0)))
        query_kv = jnp.pad(query_kv, ((0, 0), (0, rows - own), (0, 0)))
    block, columns = q_block.shape
    kv_columns = kv_block.shape[2]
    kv_heads = kv_columns // HD
    group = columns // kv_columns
    share = anchor_kv.shape[1]
    cache_count = cache_kv.shape[1]
    total = n * rows
    tile = total * max(1, min(group, 512 // total))
    extra = -(-(block + share + HD) // HD) * HD
    far = (n - 1) * share
    bf16, f32 = jnp.bfloat16, jnp.float32
    vmem = pltpu.VMEM
    dma = pltpu.SemaphoreType.DMA
    hbm = pl.BlockSpec(memory_space=pl.ANY)
    smem = pl.BlockSpec(memory_space=pltpu.SMEM)
    results = (
        jax.ShapeDtypeStruct((block, columns), bf16),
        jax.ShapeDtypeStruct((rows, columns), bf16),
    )
    block_out, query_out = pl.pallas_call(
        functools.partial(kernel, n, own),
        out_shape=results,
        in_specs=[smem] + [hbm] * 7,
        out_specs=(hbm, pl.BlockSpec(memory_space=vmem)),
        scratch_shapes=[
            pltpu.SMEM((1,), jnp.int32),
            vmem((block, columns), bf16),
            vmem((2, block, kv_columns), bf16),
            vmem((2, cache_count, kv_columns), bf16),
            vmem((2, rows, kv_columns), bf16),
            vmem((n, 2, share, kv_columns), bf16),
            vmem((total, columns), bf16),
            vmem((tile, HD), bf16),
            vmem((kv_heads, extra, HD), bf16),
            vmem((kv_heads, extra, HD), bf16),
            vmem((cache_count, HD), bf16),
            vmem((total, HD), f32),
            vmem((tile, cache_count + extra), f32),
            vmem((tile, HD), f32),
            vmem((tile, 2 * HD), f32),
            vmem((kv_heads, far, HD), bf16),
            vmem((kv_heads, far, 2 * HD), bf16),
            vmem((block, block), f32),
            vmem((columns // HD, block, HD), f32),
            vmem((columns // HD, block, 2 * HD), f32),
            vmem((block, columns), bf16),
            vmem((total, columns), bf16),
            vmem((2, total, HD), f32),
            vmem((n, rows, columns), bf16),
            vmem((n, 2, rows, HD), f32),
            dma((7,)), dma((kv_heads,)),
            dma((kv_heads, n)), dma((kv_heads, n)),
            dma((n,)), dma((n,)),
            dma((kv_heads, n)), dma((kv_heads, n)),
            dma((n,)), dma((n,)),
        ],
        compiler_params=pltpu.CompilerParams(
            collective_id=0, has_side_effects=True, vmem_limit_bytes=56 * 1024 * 1024
        ),
    )(query_pos, cache_len, q_block, kv_block, anchor_kv, cache_kv, query_q, query_kv)
    block_out, query_out = pl.pallas_call(
        hand_on,
        out_shape=results,
        in_specs=[hbm, hbm],
        out_specs=(hbm, hbm),
        scratch_shapes=[dma((2,))],
    )(block_out, query_out)
    return block_out, query_out[:own]


def solution(mesh):
    in_specs = (
        P(("groups", "ctx"), "head"),
        P(None, ("groups", "ctx"), "head"),
        P(None, ("groups", "ctx"), "head"),
        P(None, ("groups", "ctx"), "head"),
        P(("groups", "ctx")),
        P(("groups", "ctx"), "head"),
        P(None, ("groups", "ctx"), "head"),
        P("groups"),
    )
    out_specs = (P(("groups", "ctx"), "head"), P(("groups", "ctx"), "head"))
    return jax.shard_map(
        functools.partial(local, mesh.shape["ctx"]),
        mesh=mesh, in_specs=in_specs, out_specs=out_specs, check_vma=False)
```

```python
import functools
import math

import jax
import jax.numpy as jnp
from jax import lax
from jax.experimental import pallas as pl
from jax.experimental.pallas import tpu as pltpu
from jax.sharding import PartitionSpec as P

HD = 128
NEG = -1e30
SCALE2 = math.log2(math.e) / math.sqrt(HD)
CHUNK = 1024
TRIM = 256
STACK = 2
PIECES = 4
MESH = pl.DeviceIdType.MESH


def scores(queries, keys):
    dims = (((1,), (1,)), ((), ()))
    return lax.dot_general(queries, keys, dims, preferred_element_type=jnp.float32) * SCALE2


def with_ones(values):
    return jnp.concatenate([values, jnp.ones_like(values)], axis=1)


def weighted(weights, values):
    return jnp.dot(weights.astype(jnp.bfloat16), values, preferred_element_type=jnp.float32)


def kernel(
    n, own,
    pos_ref, len_hbm, q_hbm, kv_hbm, anchor_hbm, cache_hbm, qq_hbm, qkv_hbm,
    out_hbm, qout_ref,
    len_ref, q_buf, kv_buf, cache_buf, qkv_buf, anchors, queries,
    qg, kx, vx, ones, xbias, s_buf, m_run, acc, kb, vb, causal, m_blk, o_blk, out_buf,
    send_o, send_st, recv_o, recv_st,
    in_sem, out_sem, q_send, q_recv, a_send, a_recv, o_send, o_recv, st_send, st_recv,
):
    me = lax.axis_index("ctx")
    peers = [lax.rem(me + k, n) for k in range(1, n)]
    rows = qq_hbm.shape[0]
    block = q_buf.shape[0]
    columns = q_buf.shape[1]
    kv_heads = kv_buf.shape[2] // HD
    group = columns // HD // kv_heads
    share = anchor_hbm.shape[1]
    cache_count = cache_buf.shape[1]
    total = n * rows
    extra = kx.shape[1]
    tile = s_buf.shape[0]
    tile_heads = tile // total
    half = group * HD
    near_keys = block + share

    def rows_of(who):
        return pl.ds(pl.multiple_of(who * rows, rows), rows)

    def half_of(g):
        return pl.ds(pl.multiple_of(g * half, half), half)

    loads = [
        pltpu.make_async_copy(qq_hbm, queries.at[rows_of(me)], in_sem.at[0]),
        pltpu.make_async_copy(anchor_hbm, anchors.at[me], in_sem.at[1]),
        pltpu.make_async_copy(kv_hbm, kv_buf, in_sem.at[2]),
        pltpu.make_async_copy(qkv_hbm, qkv_buf, in_sem.at[3]),
        pltpu.make_async_copy(q_hbm, q_buf, in_sem.at[4]),
        pltpu.make_async_copy(len_hbm, len_ref, in_sem.at[5]),
    ]
    cache_load = pltpu.make_async_copy(cache_hbm, cache_buf, in_sem.at[6])
    for load in loads:
        load.start()
    cache_load.start()

    barrier = pltpu.get_barrier_semaphore()
    for peer in peers:
        pl.semaphore_signal(barrier, inc=1, device_id={"ctx": peer}, device_id_type=MESH)
    pl.semaphore_wait(barrier, n - 1)

    def query_copy(g, slot, peer):
        return pltpu.make_async_remote_copy(
            src_ref=qq_hbm.at[:, half_of(g)], dst_ref=queries.at[rows_of(slot), half_of(g)],
            send_sem=q_send.at[g, peer], recv_sem=q_recv.at[g, slot],
            device_id={"ctx": peer}, device_id_type=MESH)

    def anchor_copy(slot, peer):
        return pltpu.make_async_remote_copy(
            src_ref=anchor_hbm, dst_ref=anchors.at[slot], send_sem=a_send.at[peer],
            recv_sem=a_recv.at[slot], device_id={"ctx": peer}, device_id_type=MESH)

    def output_copy(g, slot, peer):
        return pltpu.make_async_remote_copy(
            src_ref=send_o.at[rows_of(peer), half_of(g)],
            dst_ref=recv_o.at[slot, :, half_of(g)], send_sem=o_send.at[g, peer],
            recv_sem=o_recv.at[g, slot], device_id={"ctx": peer}, device_id_type=MESH)

    def stats_copy(slot, peer):
        return pltpu.make_async_remote_copy(
            src_ref=send_st.at[:, rows_of(peer)],
            dst_ref=recv_st.at[slot], send_sem=st_send.at[peer],
            recv_sem=st_recv.at[slot], device_id={"ctx": peer}, device_id_type=MESH)

    for g in range(kv_heads):
        for peer in peers:
            query_copy(g, me, peer).start()

    row = lax.broadcasted_iota(jnp.int32, (total, HD), 0)
    lane = lax.broadcasted_iota(jnp.int32, (total, HD), 1)
    row_pos = jnp.zeros((total, HD), jnp.int32)
    for i in range(n * own):
        row_pos = jnp.where(row == (i // own) * rows + i % own, pos_ref[i], row_pos)
    key_pos = jnp.full((total, HD), 1 << 30, jnp.int32)
    for j in range(own):
        key_pos = jnp.where(lane == j, pos_ref[me * own + j], key_pos)
    xbias[...] = jnp.where(key_pos <= row_pos, 0.0, NEG)
    send_st[...] = jnp.zeros_like(send_st)
    first = lax.broadcasted_iota(jnp.int32, (block, block), 0)
    second = lax.broadcasted_iota(jnp.int32, (block, block), 1)
    causal[...] = jnp.where(second <= first, 0.0, NEG)

    for load in loads:
        load.wait()
    for g in range(kv_heads):
        cols = slice(g * HD, (g + 1) * HD)
        for index, target in ((0, kx), (1, vx)):
            target[g, 0:block] = kv_buf[index, :, cols]
            target[g, pl.ds(block, share)] = anchors[me, index, :, cols]
            target[g, pl.ds(near_keys, rows)] = qkv_buf[index, :, cols]
            rest = extra - near_keys - rows
            if rest:
                target[g, pl.ds(near_keys + rows, rest)] = jnp.zeros((rest, HD), jnp.bfloat16)

    def fold(block_scores):
        parts = [block_scores[:, k:k + HD] for k in range(0, block_scores.shape[1], HD)]
        return functools.reduce(jnp.maximum, parts)

    def less(block_scores, peak):
        parts = [block_scores[:, k:k + HD] - peak for k in range(0, block_scores.shape[1], HD)]
        return jnp.concatenate(parts, axis=1)

    def stacked_queries(i):
        parts = []
        for j in range(STACK):
            at = pl.multiple_of((i * STACK + j) * HD, HD)
            parts.append(q_buf[:, pl.ds(at, HD)])
        return jnp.concatenate(parts, axis=0)

    def near_heads(i, carry):
        g = i * STACK // group
        part = scores(stacked_queries(i), kx[g, pl.ds(0, near_keys)])
        hidden = jnp.concatenate([causal[...]] * STACK, axis=0)
        part = jnp.concatenate([part[:, :block] + hidden, part[:, block:]], axis=1)
        peak = jnp.max(part, axis=1, keepdims=True)
        m_blk[i] = jnp.broadcast_to(peak, (STACK * block, HD))
        o_blk[i] = weighted(jnp.exp2(part - peak), with_ones(vx[g, pl.ds(0, near_keys)]))
        return carry

    lax.fori_loop(0, columns // HD // STACK, near_heads, 0)

    for peer in peers:
        anchor_copy(me, peer).start()

    length = len_ref[0]
    cache_load.wait()
    spare = kv_buf[0, 0:16, :][0:1]
    wide = cache_buf.shape[2]

    def trim(i, carry):
        at = pl.multiple_of(i * TRIM, TRIM)
        slot = lax.broadcasted_iota(jnp.int32, (TRIM, wide), 0) + at
        visible = jnp.where(slot < length, 1.0, 0.0).astype(jnp.bfloat16)
        keys = cache_buf[0, pl.ds(at, TRIM)]
        cache_buf[0, pl.ds(at, TRIM)] = keys * visible + spare * (1.0 - visible)
        cache_buf[1, pl.ds(at, TRIM)] = cache_buf[1, pl.ds(at, TRIM)] * visible
        ones[pl.ds(at, TRIM)] = visible[:, :HD]
        return carry

    lax.fori_loop(0, cache_count // TRIM, trim, 0)

    def one_kv_head(g, carry):
        cols = pl.ds(pl.multiple_of(g * HD, HD), HD)
        for peer in peers:
            query_copy(g, peer, peer).wait_recv()

        def one_tile(t, carry):
            for j in range(tile_heads):
                head = g * group + t * tile_heads + j
                qg[j * total:(j + 1) * total] = queries[:, pl.ds(pl.multiple_of(head * HD, HD), HD)]
            near = scores(qg[...], kx[g])
            tail = jnp.concatenate([xbias[...]] * tile_heads, axis=0)
            near_parts = [near[:, :near_keys], near[:, near_keys:near_keys + HD] + tail]
            if extra > near_keys + HD:
                near_parts.append(jnp.full((tile, extra - near_keys - HD), NEG, jnp.float32))
            near = jnp.concatenate(near_parts, axis=1)
            s_buf[:, cache_count:] = near
            m_run[...] = fold(near)

            def cached_scores(i, carry):
                at = pl.multiple_of(i * CHUNK, CHUNK)
                part = scores(qg[...], cache_buf[0, pl.ds(at, CHUNK), cols])
                s_buf[:, pl.ds(at, CHUNK)] = part
                m_run[...] = jnp.maximum(m_run[...], fold(part))
                return carry

            lax.fori_loop(0, cache_count // CHUNK, cached_scores, 0)
            peak = jnp.max(m_run[...], axis=1, keepdims=True)
            m_run[...] = jnp.broadcast_to(peak, m_run.shape)
            weights = jnp.exp2(less(s_buf[:, cache_count:], m_run[...]))
            acc[...] = weighted(weights, with_ones(vx[g]))

            def cached_values(i, carry):
                at = pl.multiple_of(i * CHUNK, CHUNK)
                weights = jnp.exp2(less(s_buf[:, pl.ds(at, CHUNK)], m_run[...]))
                values = jnp.concatenate(
                    [cache_buf[1, pl.ds(at, CHUNK), cols], ones[pl.ds(at, CHUNK)]], axis=1)
                acc[...] += weighted(weights, values)
                return carry

            lax.fori_loop(0, cache_count // CHUNK, cached_values, 0)
            for j in range(tile_heads):
                head = g * group + t * tile_heads + j
                span = slice(j * total, (j + 1) * total)
                send_o[:, pl.ds(pl.multiple_of(head * HD, HD), HD)] = acc[span, :HD].astype(jnp.bfloat16)
                send_st[0] = jnp.where(lane == head, m_run[span], send_st[0])
                send_st[1] = jnp.where(lane == head, acc[span, HD:], send_st[1])
            return carry

        if group == tile_heads:
            one_tile(0, 0)
        else:
            lax.fori_loop(0, group // tile_heads, one_tile, 0)
        for peer in peers:
            output_copy(g, me, peer).start()
        return carry

    lax.fori_loop(0, kv_heads, one_kv_head, 0)
    for peer in peers:
        stats_copy(me, peer).start()

    for peer in peers:
        anchor_copy(peer, peer).wait_recv()
    for g in range(kv_heads):
        cols = slice(g * HD, (g + 1) * HD)
        for k, peer in enumerate(peers):
            kb[g, k * share:(k + 1) * share] = anchors[peer, 0, :, cols]
            vb[g, k * share:(k + 1) * share] = with_ones(anchors[peer, 1, :, cols])

    def far_heads(i, carry):
        g = i * STACK // group
        part = scores(stacked_queries(i), kb[g])
        before = m_blk[i]
        peak = jnp.maximum(before, jnp.max(part, axis=1, keepdims=True))
        result = weighted(jnp.exp2(part - peak[:, 0:1] if part.shape[1] % HD else less(part, peak)), vb[g])
        factor = jnp.exp2(before - peak)
        top = result[:, :HD] + o_blk[i, :, :HD] * factor
        below = result[:, HD:] + o_blk[i, :, HD:] * factor
        final = (top / below).astype(jnp.bfloat16)
        for j in range(STACK):
            at = pl.multiple_of((i * STACK + j) * HD, HD)
            out_buf[:, pl.ds(at, HD)] = final[j * block:(j + 1) * block]
        return carry

    steps = group // STACK
    for g in range(kv_heads):
        lax.fori_loop(g * steps, (g + 1) * steps, far_heads, 0)
        pltpu.make_async_copy(out_buf.at[:, half_of(g)], out_hbm.at[:, half_of(g)], out_sem.at[g]).start()

    for peer in peers:
        stats_copy(peer, peer).wait_recv()
        for g in range(kv_heads):
            output_copy(g, peer, peer).wait_recv()
    mine = rows_of(me)
    recv_st[me] = send_st[:, mine]
    recv_o[me] = send_o[mine]
    top = functools.reduce(jnp.maximum, [recv_st[c, 0] for c in range(n)])
    factors = [jnp.exp2(recv_st[c, 0] - top) for c in range(n)]
    whole = sum(factors[c] * recv_st[c, 1] for c in range(n))
    heads = columns // HD
    for h in range(heads):
        span = slice(h * HD, (h + 1) * HD)
        merged = sum(
            recv_o[c, :, span].astype(jnp.float32) * factors[c][:, h:h + 1] for c in range(n)
        )
        qout_ref[:, span] = (merged / whole[:, h:h + 1]).astype(jnp.bfloat16)

    for g in range(kv_heads):
        pltpu.make_async_copy(out_buf.at[:, half_of(g)], out_hbm.at[:, half_of(g)], out_sem.at[g]).wait()
    for peer in peers:
        anchor_copy(me, peer).wait_send()
        stats_copy(me, peer).wait_send()
        for g in range(kv_heads):
            query_copy(g, me, peer).wait_send()
            output_copy(g, me, peer).wait_send()


def hand_on(block_in, query_in, block_out, query_out, block_buf, query_buf, in_sems, out_sems):
    step = block_in.shape[0] // PIECES
    parts = [(query_in, query_buf, query_out)]
    for k in range(PIECES):
        span = pl.ds(k * step, step)
        parts.append((block_in.at[span], block_buf.at[span], block_out.at[span]))
    loads = [pltpu.make_async_copy(a, b, in_sems.at[k]) for k, (a, b, c) in enumerate(parts)]
    stores = [pltpu.make_async_copy(b, c, out_sems.at[k]) for k, (a, b, c) in enumerate(parts)]
    for load in loads:
        load.start()
    for load, store in zip(loads, stores):
        load.wait()
        store.start()
    for store in stores:
        store.wait()


def local(n, q_block, kv_block, anchor_kv, cache_kv, cache_len, query_q, query_kv, query_pos):
    own = query_q.shape[0]
    rows = -(-own // 16) * 16
    if rows != own:
        query_q = jnp.pad(query_q, ((0, rows - own), (0, 0)))
        query_kv = jnp.pad(query_kv, ((0, 0), (0, rows - own), (0, 0)))
    block, columns = q_block.shape
    kv_columns = kv_block.shape[2]
    kv_heads = kv_columns // HD
    group = columns // kv_columns
    share = anchor_kv.shape[1]
    cache_count = cache_kv.shape[1]
    total = n * rows
    tile = total * max(1, min(group, 512 // total))
    extra = -(-(block + share + HD) // HD) * HD
    far = (n - 1) * share
    bf16, f32 = jnp.bfloat16, jnp.float32
    vmem = pltpu.VMEM
    dma = pltpu.SemaphoreType.DMA
    hbm = pl.BlockSpec(memory_space=pl.ANY)
    smem = pl.BlockSpec(memory_space=pltpu.SMEM)
    results = (
        jax.ShapeDtypeStruct((block, columns), bf16),
        jax.ShapeDtypeStruct((rows, columns), bf16),
    )
    block_out, query_out = pl.pallas_call(
        functools.partial(kernel, n, own),
        out_shape=results,
        in_specs=[smem] + [hbm] * 7,
        out_specs=(hbm, pl.BlockSpec(memory_space=vmem)),
        scratch_shapes=[
            pltpu.SMEM((1,), jnp.int32),
            vmem((block, columns), bf16),
            vmem((2, block, kv_columns), bf16),
            vmem((2, cache_count, kv_columns), bf16),
            vmem((2, rows, kv_columns), bf16),
            vmem((n, 2, share, kv_columns), bf16),
            vmem((total, columns), bf16),
            vmem((tile, HD), bf16),
            vmem((kv_heads, extra, HD), bf16),
            vmem((kv_heads, extra, HD), bf16),
            vmem((cache_count, HD), bf16),
            vmem((total, HD), f32),
            vmem((tile, cache_count + extra), f32),
            vmem((tile, HD), f32),
            vmem((tile, 2 * HD), f32),
            vmem((kv_heads, far, HD), bf16),
            vmem((kv_heads, far, 2 * HD), bf16),
            vmem((block, block), f32),
            vmem((columns // HD // STACK, STACK * block, HD), f32),
            vmem((columns // HD // STACK, STACK * block, 2 * HD), f32),
            vmem((block, columns), bf16),
            vmem((total, columns), bf16),
            vmem((2, total, HD), f32),
            vmem((n, rows, columns), bf16),
            vmem((n, 2, rows, HD), f32),
            dma((7,)), dma((kv_heads,)),
            dma((kv_heads, n)), dma((kv_heads, n)),
            dma((n,)), dma((n,)),
            dma((kv_heads, n)), dma((kv_heads, n)),
            dma((n,)), dma((n,)),
        ],
        compiler_params=pltpu.CompilerParams(
            collective_id=0, has_side_effects=True, vmem_limit_bytes=56 * 1024 * 1024
        ),
    )(query_pos, cache_len, q_block, kv_block, anchor_kv, cache_kv, query_q, query_kv)
    block_out, query_out = pl.pallas_call(
        hand_on,
        out_shape=results,
        in_specs=[hbm, hbm],
        out_specs=(hbm, hbm),
        scratch_shapes=[
            vmem((block, columns), bf16), vmem((rows, columns), bf16), dma((PIECES + 1,)), dma((PIECES + 1,)),
        ],
    )(block_out, query_out)
    return block_out, query_out[:own]


def solution(mesh):
    in_specs = (
        P(("groups", "ctx"), "head"),
        P(None, ("groups", "ctx"), "head"),
        P(None, ("groups", "ctx"), "head"),
        P(None, ("groups", "ctx"), "head"),
        P(("groups", "ctx")),
        P(("groups", "ctx"), "head"),
        P(None, ("groups", "ctx"), "head"),
        P("groups"),
    )
    out_specs = (P(("groups", "ctx"), "head"), P(("groups", "ctx"), "head"))
    return jax.shard_map(
        functools.partial(local, mesh.shape["ctx"]),
        mesh=mesh, in_specs=in_specs, out_specs=out_specs, check_vma=False)
```

```python
import functools
import math

import jax
import jax.numpy as jnp
from jax import lax
from jax.experimental import pallas as pl
from jax.experimental.pallas import tpu as pltpu
from jax.sharding import PartitionSpec as P

HD = 128
NEG = -1e30
SCALE2 = math.log2(math.e) / math.sqrt(HD)
CHUNK = 1024
TRIM = 256
STACK = 2
PIECES = 4
MESH = pl.DeviceIdType.MESH


def scores(queries, keys):
    dims = (((1,), (1,)), ((), ()))
    return lax.dot_general(queries, keys, dims, preferred_element_type=jnp.float32) * SCALE2


def with_ones(values):
    return jnp.concatenate([values, jnp.ones_like(values)], axis=1)


def weighted(weights, values):
    return jnp.dot(weights.astype(jnp.bfloat16), values, preferred_element_type=jnp.float32)


def kernel(
    n, own,
    pos_hbm, len_hbm, q_hbm, kv_hbm, anchor_hbm, cache_hbm, qq_hbm, qkv_hbm,
    out_hbm, qout_ref,
    pos_ref, len_ref, q_buf, kv_buf, cache_buf, qkv_buf, anchors, queries,
    qg, kx, vx, ones, xbias, s_bufs, m_runs, acc, kb, vb, causal, s_near, s_far, m_pair, m_blk, o_blk, out_buf,
    send_o, send_st, recv_o, recv_st,
    in_sem, out_sem, q_send, q_recv, a_send, a_recv, o_send, o_recv, st_send, st_recv,
):
    me = lax.axis_index("ctx")
    peers = [lax.rem(me + k, n) for k in range(1, n)]
    rows = qq_hbm.shape[0]
    block = q_buf.shape[0]
    columns = q_buf.shape[1]
    kv_heads = kv_buf.shape[2] // HD
    group = columns // HD // kv_heads
    share = anchor_hbm.shape[1]
    cache_count = cache_buf.shape[1]
    total = n * rows
    extra = kx.shape[1]
    tile = acc.shape[0]
    tile_heads = tile // total
    half = group * HD
    near_keys = block + share

    def rows_of(who):
        return pl.ds(pl.multiple_of(who * rows, rows), rows)

    def half_of(g):
        return pl.ds(pl.multiple_of(g * half, half), half)

    loads = [
        pltpu.make_async_copy(qq_hbm, queries.at[rows_of(me)], in_sem.at[0]),
        pltpu.make_async_copy(anchor_hbm, anchors.at[me], in_sem.at[1]),
        pltpu.make_async_copy(kv_hbm, kv_buf, in_sem.at[2]),
        pltpu.make_async_copy(qkv_hbm, qkv_buf, in_sem.at[3]),
        pltpu.make_async_copy(q_hbm, q_buf, in_sem.at[4]),
        pltpu.make_async_copy(len_hbm, len_ref, in_sem.at[5]),
        pltpu.make_async_copy(pos_hbm, pos_ref, in_sem.at[7]),
    ]
    cache_load = pltpu.make_async_copy(cache_hbm, cache_buf, in_sem.at[6])
    for load in loads:
        load.start()
    cache_load.start()

    barrier = pltpu.get_barrier_semaphore()
    for peer in peers:
        pl.semaphore_signal(barrier, inc=1, device_id={"ctx": peer}, device_id_type=MESH)
    pl.semaphore_wait(barrier, n - 1)

    def query_copy(g, slot, peer):
        return pltpu.make_async_remote_copy(
            src_ref=qq_hbm.at[:, half_of(g)], dst_ref=queries.at[rows_of(slot), half_of(g)],
            send_sem=q_send.at[g, peer], recv_sem=q_recv.at[g, slot],
            device_id={"ctx": peer}, device_id_type=MESH)

    def anchor_copy(slot, peer):
        return pltpu.make_async_remote_copy(
            src_ref=anchor_hbm, dst_ref=anchors.at[slot], send_sem=a_send.at[peer],
            recv_sem=a_recv.at[slot], device_id={"ctx": peer}, device_id_type=MESH)

    def output_copy(g, slot, peer):
        return pltpu.make_async_remote_copy(
            src_ref=send_o.at[rows_of(peer), half_of(g)],
            dst_ref=recv_o.at[slot, :, half_of(g)], send_sem=o_send.at[g, peer],
            recv_sem=o_recv.at[g, slot], device_id={"ctx": peer}, device_id_type=MESH)

    def stats_copy(slot, peer):
        return pltpu.make_async_remote_copy(
            src_ref=send_st.at[:, rows_of(peer)],
            dst_ref=recv_st.at[slot], send_sem=st_send.at[peer],
            recv_sem=st_recv.at[slot], device_id={"ctx": peer}, device_id_type=MESH)

    for g in range(kv_heads):
        for peer in peers:
            query_copy(g, me, peer).start()

    for load in loads:
        load.wait()

    row = lax.broadcasted_iota(jnp.int32, (total, HD), 0)
    lane = lax.broadcasted_iota(jnp.int32, (total, HD), 1)
    row_pos = jnp.zeros((total, HD), jnp.int32)
    for i in range(n * own):
        row_pos = jnp.where(row == (i // own) * rows + i % own, pos_ref[i], row_pos)
    key_pos = jnp.full((total, HD), 1 << 30, jnp.int32)
    for j in range(own):
        key_pos = jnp.where(lane == j, pos_ref[me * own + j], key_pos)
    xbias[...] = jnp.where(key_pos <= row_pos, 0.0, NEG)
    send_st[...] = jnp.zeros_like(send_st)
    first = lax.broadcasted_iota(jnp.int32, (block, block), 0)
    second = lax.broadcasted_iota(jnp.int32, (block, block), 1)
    causal[...] = jnp.where(second <= first, 0.0, NEG)

    for g in range(kv_heads):
        cols = slice(g * HD, (g + 1) * HD)
        for index, target in ((0, kx), (1, vx)):
            target[g, 0:block] = kv_buf[index, :, cols]
            target[g, pl.ds(block, share)] = anchors[me, index, :, cols]
            target[g, pl.ds(near_keys, rows)] = qkv_buf[index, :, cols]
            rest = extra - near_keys - rows
            if rest:
                target[g, pl.ds(near_keys + rows, rest)] = jnp.zeros((rest, HD), jnp.bfloat16)

    def fold(block_scores):
        parts = [block_scores[:, k:k + HD] for k in range(0, block_scores.shape[1], HD)]
        return functools.reduce(jnp.maximum, parts)

    def less(block_scores, peak):
        if block_scores.shape[1] % HD:
            return block_scores - peak[:, 0:1]
        parts = [block_scores[:, k:k + HD] - peak for k in range(0, block_scores.shape[1], HD)]
        return jnp.concatenate(parts, axis=1)

    def stacked_queries(i):
        parts = []
        for j in range(STACK):
            at = pl.multiple_of((i * STACK + j) * HD, HD)
            parts.append(q_buf[:, pl.ds(at, HD)])
        return jnp.concatenate(parts, axis=0)

    steps = columns // HD // STACK

    def pipelined(first_step, count, begin, finish):
        begin(first_step, 0)

        def two_steps(k, carry):
            i = first_step + 2 * k
            begin(i + 1, 1)
            finish(i, 0)
            begin((i + 2) % steps, 0)
            finish(i + 1, 1)
            return carry

        lax.fori_loop(0, count // 2, two_steps, 0)

    def begin_near(i, slot):
        g = i * STACK // group
        part = scores(stacked_queries(i), kx[g, pl.ds(0, near_keys)])
        hidden = jnp.concatenate([causal[...]] * STACK, axis=0)
        part = jnp.concatenate([part[:, :block] + hidden, part[:, block:]], axis=1)
        s_near[slot][...] = part
        m_pair[slot][...] = jnp.broadcast_to(jnp.max(part, axis=1, keepdims=True), m_pair[slot].shape)

    def finish_near(i, slot):
        g = i * STACK // group
        m_blk[i] = m_pair[slot][...]
        weights = jnp.exp2(less(s_near[slot][...], m_pair[slot][...]))
        o_blk[i] = weighted(weights, with_ones(vx[g, pl.ds(0, near_keys)]))

    pipelined(0, steps, begin_near, finish_near)

    for peer in peers:
        anchor_copy(me, peer).start()

    length = len_ref[0]
    cache_load.wait()
    spare = kv_buf[0, 0:16, :][0:1]
    wide = cache_buf.shape[2]

    def trim(i, carry):
        at = pl.multiple_of(i * TRIM, TRIM)
        slot = lax.broadcasted_iota(jnp.int32, (TRIM, wide), 0) + at
        visible = jnp.where(slot < length, 1.0, 0.0).astype(jnp.bfloat16)
        keys = cache_buf[0, pl.ds(at, TRIM)]
        cache_buf[0, pl.ds(at, TRIM)] = keys * visible + spare * (1.0 - visible)
        cache_buf[1, pl.ds(at, TRIM)] = cache_buf[1, pl.ds(at, TRIM)] * visible
        ones[pl.ds(at, TRIM)] = visible[:, :HD]
        return carry

    lax.fori_loop(0, cache_count // TRIM, trim, 0)

    tiles = group // tile_heads
    items = [(g, t) for g in range(kv_heads) for t in range(tiles)]

    def open_item(k):
        g, t = items[k]
        s_buf, m_run, rows_in = s_bufs[k % 2], m_runs[k % 2], qg[k % 2]
        if t == 0:
            for peer in peers:
                query_copy(g, peer, peer).wait_recv()
        for j in range(tile_heads):
            head = g * group + t * tile_heads + j
            rows_in[j * total:(j + 1) * total] = queries[:, head * HD:(head + 1) * HD]
        near = scores(rows_in[...], kx[g])
        tail = jnp.concatenate([xbias[...]] * tile_heads, axis=0)
        near_parts = [near[:, :near_keys], near[:, near_keys:near_keys + HD] + tail]
        if extra > near_keys + HD:
            near_parts.append(jnp.full((tile, extra - near_keys - HD), NEG, jnp.float32))
        near = jnp.concatenate(near_parts, axis=1)
        s_buf[:, cache_count:] = near
        m_run[...] = fold(near)

    def cached_scores(k, at):
        g = items[k][0]
        s_buf, m_run, rows_in = s_bufs[k % 2], m_runs[k % 2], qg[k % 2]
        part = scores(rows_in[...], cache_buf[0, pl.ds(at, CHUNK), g * HD:(g + 1) * HD])
        s_buf[:, pl.ds(at, CHUNK)] = part
        m_run[...] = jnp.maximum(m_run[...], fold(part))

    def near_values(k):
        g = items[k][0]
        s_buf, m_run = s_bufs[k % 2], m_runs[k % 2]
        peak = jnp.max(m_run[...], axis=1, keepdims=True)
        m_run[...] = jnp.broadcast_to(peak, m_run.shape)
        acc[...] = weighted(jnp.exp2(less(s_buf[:, cache_count:], m_run[...])), with_ones(vx[g]))

    def cached_values(k, at):
        g = items[k][0]
        s_buf, m_run = s_bufs[k % 2], m_runs[k % 2]
        weights = jnp.exp2(less(s_buf[:, pl.ds(at, CHUNK)], m_run[...]))
        values = jnp.concatenate(
            [cache_buf[1, pl.ds(at, CHUNK), g * HD:(g + 1) * HD], ones[pl.ds(at, CHUNK)]], axis=1)
        acc[...] += weighted(weights, values)

    def close_item(k):
        g, t = items[k]
        m_run = m_runs[k % 2]
        for j in range(tile_heads):
            head = g * group + t * tile_heads + j
            span = slice(j * total, (j + 1) * total)
            send_o[:, head * HD:(head + 1) * HD] = acc[span, :HD].astype(jnp.bfloat16)
            send_st[0] = jnp.where(lane == head, m_run[span], send_st[0])
            send_st[1] = jnp.where(lane == head, acc[span, HD:], send_st[1])
        if t == tiles - 1:
            for peer in peers:
                output_copy(g, me, peer).start()

    for k in range(len(items) + 1):
        if k < len(items):
            open_item(k)
        if k > 0:
            near_values(k - 1)

        def one_chunk(i, carry, k=k):
            at = pl.multiple_of(i * CHUNK, CHUNK)
            if k < len(items):
                cached_scores(k, at)
            if k > 0:
                cached_values(k - 1, at)
            return carry

        lax.fori_loop(0, cache_count // CHUNK, one_chunk, 0)
        if k > 0:
            close_item(k - 1)
    for peer in peers:
        stats_copy(me, peer).start()

    for peer in peers:
        anchor_copy(peer, peer).wait_recv()
    for g in range(kv_heads):
        cols = slice(g * HD, (g + 1) * HD)
        for k, peer in enumerate(peers):
            kb[g, k * share:(k + 1) * share] = anchors[peer, 0, :, cols]
            vb[g, k * share:(k + 1) * share] = with_ones(anchors[peer, 1, :, cols])

    def begin_far(i, slot):
        part = scores(stacked_queries(i), kb[i * STACK // group])
        s_far[slot][...] = part
        m_pair[slot][...] = jnp.maximum(m_blk[i], jnp.max(part, axis=1, keepdims=True))

    def finish_far(i, slot):
        peak = m_pair[slot][...]
        result = weighted(jnp.exp2(less(s_far[slot][...], peak)), vb[i * STACK // group])
        factor = jnp.exp2(m_blk[i] - peak)
        top = result[:, :HD] + o_blk[i, :, :HD] * factor
        below = result[:, HD:] + o_blk[i, :, HD:] * factor
        final = (top / below).astype(jnp.bfloat16)
        for j in range(STACK):
            at = pl.multiple_of((i * STACK + j) * HD, HD)
            out_buf[:, pl.ds(at, HD)] = final[j * block:(j + 1) * block]

    pipelined(0, steps, begin_far, finish_far)
    for g in range(kv_heads):
        pltpu.make_async_copy(out_buf.at[:, half_of(g)], out_hbm.at[:, half_of(g)], out_sem.at[g]).start()

    for peer in peers:
        stats_copy(peer, peer).wait_recv()
        for g in range(kv_heads):
            output_copy(g, peer, peer).wait_recv()
    mine = rows_of(me)
    recv_st[me] = send_st[:, mine]
    recv_o[me] = send_o[mine]
    top = functools.reduce(jnp.maximum, [recv_st[c, 0] for c in range(n)])
    factors = [jnp.exp2(recv_st[c, 0] - top) for c in range(n)]
    whole = sum(factors[c] * recv_st[c, 1] for c in range(n))
    heads = columns // HD
    for h in range(heads):
        span = slice(h * HD, (h + 1) * HD)
        merged = sum(
            recv_o[c, :, span].astype(jnp.float32) * factors[c][:, h:h + 1] for c in range(n)
        )
        qout_ref[:, span] = (merged / whole[:, h:h + 1]).astype(jnp.bfloat16)

    for g in range(kv_heads):
        pltpu.make_async_copy(out_buf.at[:, half_of(g)], out_hbm.at[:, half_of(g)], out_sem.at[g]).wait()
    for peer in peers:
        anchor_copy(me, peer).wait_send()
        stats_copy(me, peer).wait_send()
        for g in range(kv_heads):
            query_copy(g, me, peer).wait_send()
            output_copy(g, me, peer).wait_send()


def hand_on(block_in, query_in, block_out, query_out, block_buf, query_buf, in_sems, out_sems):
    step = block_in.shape[0] // PIECES
    parts = [(query_in, query_buf, query_out)]
    for k in range(PIECES):
        span = pl.ds(k * step, step)
        parts.append((block_in.at[span], block_buf.at[span], block_out.at[span]))
    loads = [pltpu.make_async_copy(a, b, in_sems.at[k]) for k, (a, b, c) in enumerate(parts)]
    stores = [pltpu.make_async_copy(b, c, out_sems.at[k]) for k, (a, b, c) in enumerate(parts)]
    for load in loads:
        load.start()
    for load, store in zip(loads, stores):
        load.wait()
        store.start()
    for store in stores:
        store.wait()


def local(n, q_block, kv_block, anchor_kv, cache_kv, cache_len, query_q, query_kv, query_pos):
    own = query_q.shape[0]
    rows = -(-own // 16) * 16
    if rows != own:
        query_q = jnp.pad(query_q, ((0, rows - own), (0, 0)))
        query_kv = jnp.pad(query_kv, ((0, 0), (0, rows - own), (0, 0)))
    block, columns = q_block.shape
    kv_columns = kv_block.shape[2]
    kv_heads = kv_columns // HD
    group = columns // kv_columns
    share = anchor_kv.shape[1]
    cache_count = cache_kv.shape[1]
    total = n * rows
    tile = total * max(1, min(group, 512 // total))
    extra = -(-(block + share + HD) // HD) * HD
    far = (n - 1) * share
    bf16, f32 = jnp.bfloat16, jnp.float32
    vmem = pltpu.VMEM
    dma = pltpu.SemaphoreType.DMA
    hbm = pl.BlockSpec(memory_space=pl.ANY)
    stacked = STACK * block
    results = (
        jax.ShapeDtypeStruct((block, columns), bf16),
        jax.ShapeDtypeStruct((rows, columns), bf16),
    )
    block_out, query_out = pl.pallas_call(
        functools.partial(kernel, n, own),
        out_shape=results,
        in_specs=[hbm] * 8,
        out_specs=(hbm, pl.BlockSpec(memory_space=vmem)),
        scratch_shapes=[
            pltpu.SMEM(query_pos.shape, jnp.int32),
            pltpu.SMEM((1,), jnp.int32),
            vmem((block, columns), bf16),
            vmem((2, block, kv_columns), bf16),
            vmem((2, cache_count, kv_columns), bf16),
            vmem((2, rows, kv_columns), bf16),
            vmem((n, 2, share, kv_columns), bf16),
            vmem((total, columns), bf16),
            [vmem((tile, HD), bf16)] * 2,
            vmem((kv_heads, extra, HD), bf16),
            vmem((kv_heads, extra, HD), bf16),
            vmem((cache_count, HD), bf16),
            vmem((total, HD), f32),
            [vmem((tile, cache_count + extra), f32)] * 2,
            [vmem((tile, HD), f32)] * 2,
            vmem((tile, 2 * HD), f32),
            vmem((kv_heads, far, HD), bf16),
            vmem((kv_heads, far, 2 * HD), bf16),
            vmem((block, block), f32),
            [vmem((stacked, block + share), f32)] * 2,
            [vmem((stacked, far), f32)] * 2,
            [vmem((stacked, HD), f32)] * 2,
            vmem((columns // HD // STACK, STACK * block, HD), f32),
            vmem((columns // HD // STACK, STACK * block, 2 * HD), f32),
            vmem((block, columns), bf16),
            vmem((total, columns), bf16),
            vmem((2, total, HD), f32),
            vmem((n, rows, columns), bf16),
            vmem((n, 2, rows, HD), f32),
            dma((8,)), dma((kv_heads,)),
            dma((kv_heads, n)), dma((kv_heads, n)),
            dma((n,)), dma((n,)),
            dma((kv_heads, n)), dma((kv_heads, n)),
            dma((n,)), dma((n,)),
        ],
        compiler_params=pltpu.CompilerParams(
            collective_id=0, has_side_effects=True, vmem_limit_bytes=56 * 1024 * 1024
        ),
    )(query_pos, cache_len, q_block, kv_block, anchor_kv, cache_kv, query_q, query_kv)
    block_out, query_out = pl.pallas_call(
        hand_on,
        out_shape=results,
        in_specs=[hbm, hbm],
        out_specs=(hbm, hbm),
        scratch_shapes=[
            vmem((block, columns), bf16), vmem((rows, columns), bf16), dma((PIECES + 1,)), dma((PIECES + 1,)),
        ],
    )(block_out, query_out)
    return block_out, query_out[:own]


def solution(mesh):
    in_specs = (
        P(("groups", "ctx"), "head"),
        P(None, ("groups", "ctx"), "head"),
        P(None, ("groups", "ctx"), "head"),
        P(None, ("groups", "ctx"), "head"),
        P(("groups", "ctx")),
        P(("groups", "ctx"), "head"),
        P(None, ("groups", "ctx"), "head"),
        P("groups"),
    )
    out_specs = (P(("groups", "ctx"), "head"), P(("groups", "ctx"), "head"))
    return jax.shard_map(
        functools.partial(local, mesh.shape["ctx"]),
        mesh=mesh, in_specs=in_specs, out_specs=out_specs, check_vma=False)
```

```python
import functools
import math

import jax
import jax.numpy as jnp
from jax import lax
from jax.experimental import pallas as pl
from jax.experimental.pallas import tpu as pltpu
from jax.sharding import PartitionSpec as P

HD = 128
NEG = -1e30
SCALE2 = math.log2(math.e) / math.sqrt(HD)
CHUNK = 1024
TRIM = 256
STACK = 2
PIECES = 4
MESH = pl.DeviceIdType.MESH


def scores(queries, keys):
    dims = (((1,), (1,)), ((), ()))
    return lax.dot_general(queries, keys, dims, preferred_element_type=jnp.float32) * SCALE2


def with_ones(values):
    return jnp.concatenate([values, jnp.ones_like(values)], axis=1)


def weighted(weights, values):
    return jnp.dot(weights.astype(jnp.bfloat16), values, preferred_element_type=jnp.float32)


def kernel(
    n, own,
    pos_hbm, len_hbm, q_hbm, kv_hbm, anchor_hbm, cache_hbm, qq_hbm, qkv_hbm,
    out_hbm, qout_ref,
    pos_ref, len_ref, q_buf, kv_buf, cache_buf, qkv_buf, anchors, queries,
    qg, kx, vx, ones, xbias, s_bufs, m_runs, acc, kb, vb, causal, s_near, s_far, m_pair, m_blk, o_blk, out_buf,
    send_o, send_st, recv_o, recv_st,
    in_sem, out_sem, q_send, q_recv, a_send, a_recv, o_send, o_recv, st_send, st_recv,
):
    me = lax.axis_index("ctx")
    peers = [lax.rem(me + k, n) for k in range(1, n)]
    rows = qq_hbm.shape[0]
    block = q_buf.shape[0]
    columns = q_buf.shape[1]
    kv_heads = kv_buf.shape[2] // HD
    group = columns // HD // kv_heads
    share = anchor_hbm.shape[1]
    cache_count = cache_buf.shape[1]
    total = n * rows
    extra = kx.shape[1]
    tile = acc.shape[0]
    tile_heads = tile // total
    half = group * HD
    heads = columns // HD
    near_keys = block + share

    def rows_of(who):
        return pl.ds(pl.multiple_of(who * rows, rows), rows)

    def half_of(g):
        return pl.ds(pl.multiple_of(g * half, half), half)

    loads = [
        pltpu.make_async_copy(qq_hbm, queries.at[rows_of(me)], in_sem.at[0]),
        pltpu.make_async_copy(anchor_hbm, anchors.at[me], in_sem.at[1]),
        pltpu.make_async_copy(kv_hbm, kv_buf, in_sem.at[2]),
        pltpu.make_async_copy(qkv_hbm, qkv_buf, in_sem.at[3]),
        pltpu.make_async_copy(q_hbm, q_buf, in_sem.at[4]),
        pltpu.make_async_copy(len_hbm, len_ref, in_sem.at[5]),
        pltpu.make_async_copy(pos_hbm, pos_ref, in_sem.at[7]),
    ]
    cache_load = pltpu.make_async_copy(cache_hbm, cache_buf, in_sem.at[6])
    for load in loads:
        load.start()
    cache_load.start()

    barrier = pltpu.get_barrier_semaphore()
    for peer in peers:
        pl.semaphore_signal(barrier, inc=1, device_id={"ctx": peer}, device_id_type=MESH)
    pl.semaphore_wait(barrier, n - 1)

    def query_copy(g, slot, peer):
        return pltpu.make_async_remote_copy(
            src_ref=qq_hbm.at[:, half_of(g)], dst_ref=queries.at[rows_of(slot), half_of(g)],
            send_sem=q_send.at[g, peer], recv_sem=q_recv.at[g, slot],
            device_id={"ctx": peer}, device_id_type=MESH)

    ways = (1, -1)
    reach = min(2, n - 1)

    def inside(host):
        return jnp.logical_and(host >= 0, host < n)

    def anchor_direct(way, distance):
        return pltpu.make_async_remote_copy(
            src_ref=anchor_hbm, dst_ref=anchors.at[me], send_sem=a_send.at[(1 - way) // 2, distance - 1],
            recv_sem=a_recv.at[me], device_id={"ctx": me + way * distance}, device_id_type=MESH)

    def anchor_passed(way, distance):
        origin = me - way * (distance - 1)
        return pltpu.make_async_remote_copy(
            src_ref=anchors.at[origin], dst_ref=anchors.at[origin],
            send_sem=a_send.at[(1 - way) // 2, distance - 1],
            recv_sem=a_recv.at[origin], device_id={"ctx": me + way}, device_id_type=MESH)

    def for_each_direct(action):
        for distance in range(reach, 0, -1):
            for way in ways:
                @pl.when(inside(me + way * distance))
                def _():
                    action(anchor_direct(way, distance))

    def for_each_passed(action):
        for distance in range(reach + 1, n):
            for way in ways:
                @pl.when(jnp.logical_and(inside(me - way * (distance - 1)), inside(me + way)))
                def _():
                    action(way, distance)

    def pass_on(way, distance):
        copy = anchor_passed(way, distance)
        copy.wait_recv()
        copy.start()

    def wait_for_anchors():
        for distance in range(1, n):
            for way in ways:
                here = inside(me - way * distance)
                if reach <= distance < n - 1:
                    here = jnp.logical_and(here, jnp.logical_not(inside(me + way)))

                @pl.when(here)
                def _():
                    anchor_passed(way, distance + 1).wait_recv()

    def output_copy(g, slot, peer):
        return pltpu.make_async_remote_copy(
            src_ref=send_o.at[rows_of(peer), half_of(g)],
            dst_ref=recv_o.at[slot, :, half_of(g)], send_sem=o_send.at[g, peer],
            recv_sem=o_recv.at[g, slot], device_id={"ctx": peer}, device_id_type=MESH)

    def stats_copy(slot, peer):
        return pltpu.make_async_remote_copy(
            src_ref=send_st.at[rows_of(peer)],
            dst_ref=recv_st.at[slot], send_sem=st_send.at[peer],
            recv_sem=st_recv.at[slot], device_id={"ctx": peer}, device_id_type=MESH)

    for g in range(kv_heads):
        for peer in peers:
            query_copy(g, me, peer).start()

    for load in loads:
        load.wait()

    row = lax.broadcasted_iota(jnp.int32, (total, HD), 0)
    lane = lax.broadcasted_iota(jnp.int32, (total, HD), 1)
    row_pos = jnp.zeros((total, HD), jnp.int32)
    for i in range(n * own):
        row_pos = jnp.where(row == (i // own) * rows + i % own, pos_ref[i], row_pos)
    key_pos = jnp.full((total, HD), 1 << 30, jnp.int32)
    for j in range(own):
        key_pos = jnp.where(lane == j, pos_ref[me * own + j], key_pos)
    xbias[...] = jnp.where(key_pos <= row_pos, 0.0, NEG)
    send_st[...] = jnp.zeros_like(send_st)
    first = lax.broadcasted_iota(jnp.int32, (block, block), 0)
    second = lax.broadcasted_iota(jnp.int32, (block, block), 1)
    causal[...] = jnp.where(second <= first, 0.0, NEG)

    for g in range(kv_heads):
        cols = slice(g * HD, (g + 1) * HD)
        for index, target in ((0, kx), (1, vx)):
            target[g, 0:block] = kv_buf[index, :, cols]
            target[g, pl.ds(block, share)] = anchors[me, index, :, cols]
            target[g, pl.ds(near_keys, rows)] = qkv_buf[index, :, cols]
            rest = extra - near_keys - rows
            if rest:
                target[g, pl.ds(near_keys + rows, rest)] = jnp.zeros((rest, HD), jnp.bfloat16)

    def fold(block_scores):
        parts = [block_scores[:, k:k + HD] for k in range(0, block_scores.shape[1], HD)]
        return functools.reduce(jnp.maximum, parts)

    def less(block_scores, peak):
        if block_scores.shape[1] % HD:
            return block_scores - peak[:, 0:1]
        parts = [block_scores[:, k:k + HD] - peak for k in range(0, block_scores.shape[1], HD)]
        return jnp.concatenate(parts, axis=1)

    def stacked_queries(i):
        parts = []
        for j in range(STACK):
            at = pl.multiple_of((i * STACK + j) * HD, HD)
            parts.append(q_buf[:, pl.ds(at, HD)])
        return jnp.concatenate(parts, axis=0)

    steps = columns // HD // STACK

    def pipelined(first_step, count, begin, finish):
        begin(first_step, 0)

        def two_steps(k, carry):
            i = first_step + 2 * k
            begin(i + 1, 1)
            finish(i, 0)
            begin((i + 2) % steps, 0)
            finish(i + 1, 1)
            return carry

        lax.fori_loop(0, count // 2, two_steps, 0)

    def begin_near(i, slot):
        g = i * STACK // group
        part = scores(stacked_queries(i), kx[g, pl.ds(0, near_keys)])
        hidden = jnp.concatenate([causal[...]] * STACK, axis=0)
        part = jnp.concatenate([part[:, :block] + hidden, part[:, block:]], axis=1)
        s_near[slot][...] = part
        m_pair[slot][...] = jnp.broadcast_to(jnp.max(part, axis=1, keepdims=True), m_pair[slot].shape)

    def finish_near(i, slot):
        g = i * STACK // group
        m_blk[i] = m_pair[slot][...]
        weights = jnp.exp2(less(s_near[slot][...], m_pair[slot][...]))
        o_blk[i] = weighted(weights, with_ones(vx[g, pl.ds(0, near_keys)]))

    pipelined(0, steps, begin_near, finish_near)

    for_each_direct(lambda copy: copy.start())

    length = len_ref[0]
    cache_load.wait()
    spare = kv_buf[0, 0:16, :][0:1]
    wide = cache_buf.shape[2]

    def trim(i, carry):
        at = pl.multiple_of(i * TRIM, TRIM)
        slot = lax.broadcasted_iota(jnp.int32, (TRIM, wide), 0) + at
        visible = jnp.where(slot < length, 1.0, 0.0).astype(jnp.bfloat16)
        keys = cache_buf[0, pl.ds(at, TRIM)]
        cache_buf[0, pl.ds(at, TRIM)] = keys * visible + spare * (1.0 - visible)
        cache_buf[1, pl.ds(at, TRIM)] = cache_buf[1, pl.ds(at, TRIM)] * visible
        ones[pl.ds(at, TRIM)] = visible[:, :HD]
        return carry

    lax.fori_loop(0, cache_count // TRIM, trim, 0)

    tiles = group // tile_heads
    items = [(g, t) for g in range(kv_heads) for t in range(tiles)]

    def open_item(k):
        g, t = items[k]
        s_buf, m_run, rows_in = s_bufs[k % 2], m_runs[k % 2], qg[k % 2]
        if t == 0:
            for peer in peers:
                query_copy(g, peer, peer).wait_recv()
        for j in range(tile_heads):
            head = g * group + t * tile_heads + j
            rows_in[j * total:(j + 1) * total] = queries[:, head * HD:(head + 1) * HD]
        near = scores(rows_in[...], kx[g])
        tail = jnp.concatenate([xbias[...]] * tile_heads, axis=0)
        near_parts = [near[:, :near_keys], near[:, near_keys:near_keys + HD] + tail]
        if extra > near_keys + HD:
            near_parts.append(jnp.full((tile, extra - near_keys - HD), NEG, jnp.float32))
        near = jnp.concatenate(near_parts, axis=1)
        s_buf[:, cache_count:] = near
        m_run[...] = fold(near)

    def cached_scores(k, at):
        g = items[k][0]
        s_buf, m_run, rows_in = s_bufs[k % 2], m_runs[k % 2], qg[k % 2]
        part = scores(rows_in[...], cache_buf[0, pl.ds(at, CHUNK), g * HD:(g + 1) * HD])
        s_buf[:, pl.ds(at, CHUNK)] = part
        m_run[...] = jnp.maximum(m_run[...], fold(part))

    def near_values(k):
        g = items[k][0]
        s_buf, m_run = s_bufs[k % 2], m_runs[k % 2]
        peak = jnp.max(m_run[...], axis=1, keepdims=True)
        m_run[...] = jnp.broadcast_to(peak, m_run.shape)
        acc[...] = weighted(jnp.exp2(less(s_buf[:, cache_count:], m_run[...])), with_ones(vx[g]))

    def cached_values(k, at):
        g = items[k][0]
        s_buf, m_run = s_bufs[k % 2], m_runs[k % 2]
        weights = jnp.exp2(less(s_buf[:, pl.ds(at, CHUNK)], m_run[...]))
        values = jnp.concatenate(
            [cache_buf[1, pl.ds(at, CHUNK), g * HD:(g + 1) * HD], ones[pl.ds(at, CHUNK)]], axis=1)
        acc[...] += weighted(weights, values)

    def close_item(k):
        g, t = items[k]
        m_run = m_runs[k % 2]
        for j in range(tile_heads):
            head = g * group + t * tile_heads + j
            span = slice(j * total, (j + 1) * total)
            send_o[:, head * HD:(head + 1) * HD] = acc[span, :HD].astype(jnp.bfloat16)
            marked = jnp.where(lane == head, m_run[span], send_st[...])
            send_st[...] = jnp.where(lane == heads + head, acc[span, HD:], marked)
        if t == tiles - 1:
            for peer in peers:
                output_copy(g, me, peer).start()

    for k in range(len(items) + 1):
        if k < len(items):
            open_item(k)
        if k > 0:
            near_values(k - 1)

        def one_chunk(i, carry, k=k):
            at = pl.multiple_of(i * CHUNK, CHUNK)
            if k < len(items):
                cached_scores(k, at)
            if k > 0:
                cached_values(k - 1, at)
            return carry

        lax.fori_loop(0, cache_count // CHUNK, one_chunk, 0)
        if k > 0:
            close_item(k - 1)
        if k == min(1, len(items) - 1):
            for_each_passed(pass_on)
    for peer in peers:
        stats_copy(me, peer).start()

    wait_for_anchors()
    for g in range(kv_heads):
        cols = slice(g * HD, (g + 1) * HD)
        for k, peer in enumerate(peers):
            kb[g, k * share:(k + 1) * share] = anchors[peer, 0, :, cols]
            vb[g, k * share:(k + 1) * share] = with_ones(anchors[peer, 1, :, cols])

    def begin_far(i, slot):
        part = scores(stacked_queries(i), kb[i * STACK // group])
        s_far[slot][...] = part
        m_pair[slot][...] = jnp.maximum(m_blk[i], jnp.max(part, axis=1, keepdims=True))

    def finish_far(i, slot):
        peak = m_pair[slot][...]
        result = weighted(jnp.exp2(less(s_far[slot][...], peak)), vb[i * STACK // group])
        factor = jnp.exp2(m_blk[i] - peak)
        top = result[:, :HD] + o_blk[i, :, :HD] * factor
        below = result[:, HD:] + o_blk[i, :, HD:] * factor
        final = (top / below).astype(jnp.bfloat16)
        for j in range(STACK):
            at = pl.multiple_of((i * STACK + j) * HD, HD)
            out_buf[:, pl.ds(at, HD)] = final[j * block:(j + 1) * block]

    pipelined(0, steps, begin_far, finish_far)
    for g in range(kv_heads):
        pltpu.make_async_copy(out_buf.at[:, half_of(g)], out_hbm.at[:, half_of(g)], out_sem.at[g]).start()

    for peer in peers:
        stats_copy(peer, peer).wait_recv()
        for g in range(kv_heads):
            output_copy(g, peer, peer).wait_recv()
    mine = rows_of(me)
    recv_st[me] = send_st[mine]
    recv_o[me] = send_o[mine]
    top = functools.reduce(jnp.maximum, [recv_st[c] for c in range(n)])
    factors = [jnp.exp2(recv_st[c] - top) for c in range(n)]
    totals = [pltpu.roll(recv_st[c], HD - heads, 1) for c in range(n)]
    whole = sum(factors[c] * totals[c] for c in range(n))
    for h in range(heads):
        span = slice(h * HD, (h + 1) * HD)
        merged = sum(
            recv_o[c, :, span].astype(jnp.float32) * factors[c][:, h:h + 1] for c in range(n)
        )
        qout_ref[:, span] = (merged / whole[:, h:h + 1]).astype(jnp.bfloat16)

    for g in range(kv_heads):
        pltpu.make_async_copy(out_buf.at[:, half_of(g)], out_hbm.at[:, half_of(g)], out_sem.at[g]).wait()
    for_each_direct(lambda copy: copy.wait_send())
    for_each_passed(lambda way, distance: anchor_passed(way, distance).wait_send())
    for peer in peers:
        stats_copy(me, peer).wait_send()
        for g in range(kv_heads):
            query_copy(g, me, peer).wait_send()
            output_copy(g, me, peer).wait_send()


def hand_on(block_in, query_in, block_out, query_out, block_buf, query_buf, in_sems, out_sems):
    step = block_in.shape[0] // PIECES
    parts = [(query_in, query_buf, query_out)]
    for k in range(PIECES):
        span = pl.ds(k * step, step)
        parts.append((block_in.at[span], block_buf.at[span], block_out.at[span]))
    loads = [pltpu.make_async_copy(a, b, in_sems.at[k]) for k, (a, b, c) in enumerate(parts)]
    stores = [pltpu.make_async_copy(b, c, out_sems.at[k]) for k, (a, b, c) in enumerate(parts)]
    for load in loads:
        load.start()
    for load, store in zip(loads, stores):
        load.wait()
        store.start()
    for store in stores:
        store.wait()


def local(n, q_block, kv_block, anchor_kv, cache_kv, cache_len, query_q, query_kv, query_pos):
    own = query_q.shape[0]
    rows = -(-own // 16) * 16
    if rows != own:
        query_q = jnp.pad(query_q, ((0, rows - own), (0, 0)))
        query_kv = jnp.pad(query_kv, ((0, 0), (0, rows - own), (0, 0)))
    block, columns = q_block.shape
    kv_columns = kv_block.shape[2]
    kv_heads = kv_columns // HD
    group = columns // kv_columns
    share = anchor_kv.shape[1]
    cache_count = cache_kv.shape[1]
    total = n * rows
    tile = total * max(1, min(group, 512 // total))
    extra = -(-(block + share + HD) // HD) * HD
    far = (n - 1) * share
    bf16, f32 = jnp.bfloat16, jnp.float32
    vmem = pltpu.VMEM
    dma = pltpu.SemaphoreType.DMA
    hbm = pl.BlockSpec(memory_space=pl.ANY)
    stacked = STACK * block
    results = (
        jax.ShapeDtypeStruct((block, columns), bf16),
        jax.ShapeDtypeStruct((rows, columns), bf16),
    )
    block_out, query_out = pl.pallas_call(
        functools.partial(kernel, n, own),
        out_shape=results,
        in_specs=[hbm] * 8,
        out_specs=(hbm, pl.BlockSpec(memory_space=vmem)),
        scratch_shapes=[
            pltpu.SMEM(query_pos.shape, jnp.int32),
            pltpu.SMEM((1,), jnp.int32),
            vmem((block, columns), bf16),
            vmem((2, block, kv_columns), bf16),
            vmem((2, cache_count, kv_columns), bf16),
            vmem((2, rows, kv_columns), bf16),
            vmem((n, 2, share, kv_columns), bf16),
            vmem((total, columns), bf16),
            [vmem((tile, HD), bf16)] * 2,
            vmem((kv_heads, extra, HD), bf16),
            vmem((kv_heads, extra, HD), bf16),
            vmem((cache_count, HD), bf16),
            vmem((total, HD), f32),
            [vmem((tile, cache_count + extra), f32)] * 2,
            [vmem((tile, HD), f32)] * 2,
            vmem((tile, 2 * HD), f32),
            vmem((kv_heads, far, HD), bf16),
            vmem((kv_heads, far, 2 * HD), bf16),
            vmem((block, block), f32),
            [vmem((stacked, block + share), f32)] * 2,
            [vmem((stacked, far), f32)] * 2,
            [vmem((stacked, HD), f32)] * 2,
            vmem((columns // HD // STACK, STACK * block, HD), f32),
            vmem((columns // HD // STACK, STACK * block, 2 * HD), f32),
            vmem((block, columns), bf16),
            vmem((total, columns), bf16),
            vmem((total, HD), f32),
            vmem((n, rows, columns), bf16),
            vmem((n, rows, HD), f32),
            dma((8,)), dma((kv_heads,)),
            dma((kv_heads, n)), dma((kv_heads, n)),
            dma((2, n)), dma((n,)),
            dma((kv_heads, n)), dma((kv_heads, n)),
            dma((n,)), dma((n,)),
        ],
        compiler_params=pltpu.CompilerParams(
            collective_id=0, has_side_effects=True, vmem_limit_bytes=56 * 1024 * 1024
        ),
    )(query_pos, cache_len, q_block, kv_block, anchor_kv, cache_kv, query_q, query_kv)
    block_out, query_out = pl.pallas_call(
        hand_on,
        out_shape=results,
        in_specs=[hbm, hbm],
        out_specs=(hbm, hbm),
        scratch_shapes=[
            vmem((block, columns), bf16), vmem((rows, columns), bf16), dma((PIECES + 1,)), dma((PIECES + 1,)),
        ],
    )(block_out, query_out)
    return block_out, query_out[:own]


def solution(mesh):
    in_specs = (
        P(("groups", "ctx"), "head"),
        P(None, ("groups", "ctx"), "head"),
        P(None, ("groups", "ctx"), "head"),
        P(None, ("groups", "ctx"), "head"),
        P(("groups", "ctx")),
        P(("groups", "ctx"), "head"),
        P(None, ("groups", "ctx"), "head"),
        P("groups"),
    )
    out_specs = (P(("groups", "ctx"), "head"), P(("groups", "ctx"), "head"))
    return jax.shard_map(
        functools.partial(local, mesh.shape["ctx"]),
        mesh=mesh, in_specs=in_specs, out_specs=out_specs, check_vma=False)
```

```python
import functools
import math

import jax
import jax.numpy as jnp
from jax import lax
from jax.experimental import pallas as pl
from jax.experimental.pallas import tpu as pltpu
from jax.sharding import PartitionSpec as P

HD = 128
NEG = -1e30
SCALE2 = math.log2(math.e) / math.sqrt(HD)
CHUNK = 1024
TRIM = 256
STACK = 2
PIECES = 4
MESH = pl.DeviceIdType.MESH


def scores(queries, keys):
    dims = (((1,), (1,)), ((), ()))
    return lax.dot_general(queries, keys, dims, preferred_element_type=jnp.float32) * SCALE2


def with_ones(values):
    return jnp.concatenate([values, jnp.ones_like(values)], axis=1)


def weighted(weights, values):
    return jnp.dot(weights.astype(jnp.bfloat16), values, preferred_element_type=jnp.float32)


def kernel(
    n, own,
    pos_hbm, len_hbm, q_hbm, kv_hbm, anchor_hbm, cache_hbm, qq_hbm, qkv_hbm,
    out_hbm, qout_ref,
    pos_ref, len_ref, q_buf, kv_buf, cache_buf, qkv_buf, anchors, queries,
    qg, kx, vx, ones, xbias, s_bufs, m_runs, acc, kb, vb, causal, s_near, s_far, m_pair, m_blk, o_blk, out_buf,
    send_o, send_st, recv_o, recv_st,
    in_sem, out_sem, q_send, q_recv, a_send, a_recv, o_send, o_recv, st_send, st_recv,
):
    me = lax.axis_index("ctx")
    peers = [lax.rem(me + k, n) for k in range(1, n)]
    rows = qq_hbm.shape[0]
    block = q_buf.shape[0]
    columns = q_buf.shape[1]
    kv_heads = kv_buf.shape[2] // HD
    group = columns // HD // kv_heads
    share = anchor_hbm.shape[1]
    cache_count = cache_buf.shape[1]
    total = n * rows
    extra = kx.shape[1]
    tile = acc.shape[0]
    tile_heads = tile // total
    half = group * HD
    heads = columns // HD
    near_keys = block + share

    def rows_of(who):
        return pl.ds(pl.multiple_of(who * rows, rows), rows)

    def half_of(g):
        return pl.ds(pl.multiple_of(g * half, half), half)

    loads = [
        pltpu.make_async_copy(qq_hbm, queries.at[rows_of(me)], in_sem.at[0]),
        pltpu.make_async_copy(anchor_hbm, anchors.at[me], in_sem.at[1]),
        pltpu.make_async_copy(kv_hbm, kv_buf, in_sem.at[2]),
        pltpu.make_async_copy(qkv_hbm, qkv_buf, in_sem.at[3]),
        pltpu.make_async_copy(q_hbm, q_buf, in_sem.at[4]),
        pltpu.make_async_copy(len_hbm, len_ref, in_sem.at[5]),
        pltpu.make_async_copy(pos_hbm, pos_ref, in_sem.at[7]),
    ]
    cache_load = pltpu.make_async_copy(cache_hbm, cache_buf, in_sem.at[6])
    for load in loads:
        load.start()
    cache_load.start()

    barrier = pltpu.get_barrier_semaphore()
    for peer in peers:
        pl.semaphore_signal(barrier, inc=1, device_id={"ctx": peer}, device_id_type=MESH)
    pl.semaphore_wait(barrier, n - 1)

    ways = (1, -1)
    reach = min(2, n - 1)

    def inside(host):
        return jnp.logical_and(host >= 0, host < n)

    def anchor_line(slot, target, sends, direct):
        return pltpu.make_async_remote_copy(
            src_ref=anchor_hbm if direct else anchors.at[slot], dst_ref=anchors.at[slot],
            send_sem=a_send.at[sends], recv_sem=a_recv.at[slot],
            device_id={"ctx": target}, device_id_type=MESH)

    def query_line(g):
        def line(slot, target, sends, direct):
            there = queries.at[rows_of(slot), half_of(g)]
            return pltpu.make_async_remote_copy(
                src_ref=qq_hbm.at[:, half_of(g)] if direct else there, dst_ref=there,
                send_sem=q_send.at[(g,) + sends], recv_sem=q_recv.at[g, slot],
                device_id={"ctx": target}, device_id_type=MESH)
        return line

    def sender(way, distance):
        return ((1 - way) // 2, distance - 1)

    def passed(line, way, distance):
        return line(me - way * (distance - 1), me + way, sender(way, distance), False)

    def for_each_direct(line, action):
        for distance in range(reach, 0, -1):
            for way in ways:
                @pl.when(inside(me + way * distance))
                def _():
                    action(line(me, me + way * distance, sender(way, distance), True))

    def for_each_passed(line, action):
        for distance in range(reach + 1, n):
            for way in ways:
                @pl.when(jnp.logical_and(inside(me - way * (distance - 1)), inside(me + way)))
                def _():
                    action(passed(line, way, distance))

    def begin_line(line):
        for_each_direct(line, lambda copy: copy.start())

    def pass_on(line):
        def receive_and_send(copy):
            copy.wait_recv()
            copy.start()
        for_each_passed(line, receive_and_send)

    def receive(line):
        for distance in range(1, n):
            for way in ways:
                here = inside(me - way * distance)
                if reach <= distance < n - 1:
                    here = jnp.logical_and(here, jnp.logical_not(inside(me + way)))

                @pl.when(here)
                def _():
                    passed(line, way, distance + 1).wait_recv()

    def drain(line):
        for_each_direct(line, lambda copy: copy.wait_send())
        for_each_passed(line, lambda copy: copy.wait_send())

    def output_copy(g, slot, peer):
        return pltpu.make_async_remote_copy(
            src_ref=send_o.at[rows_of(peer), half_of(g)],
            dst_ref=recv_o.at[slot, :, half_of(g)], send_sem=o_send.at[g, peer],
            recv_sem=o_recv.at[g, slot], device_id={"ctx": peer}, device_id_type=MESH)

    def stats_copy(slot, peer):
        return pltpu.make_async_remote_copy(
            src_ref=send_st.at[rows_of(peer)],
            dst_ref=recv_st.at[slot], send_sem=st_send.at[peer],
            recv_sem=st_recv.at[slot], device_id={"ctx": peer}, device_id_type=MESH)

    for g in range(kv_heads):
        begin_line(query_line(g))

    for load in loads:
        load.wait()

    row = lax.broadcasted_iota(jnp.int32, (total, HD), 0)
    lane = lax.broadcasted_iota(jnp.int32, (total, HD), 1)
    row_pos = jnp.zeros((total, HD), jnp.int32)
    for i in range(n * own):
        row_pos = jnp.where(row == (i // own) * rows + i % own, pos_ref[i], row_pos)
    key_pos = jnp.full((total, HD), 1 << 30, jnp.int32)
    for j in range(own):
        key_pos = jnp.where(lane == j, pos_ref[me * own + j], key_pos)
    xbias[...] = jnp.where(key_pos <= row_pos, 0.0, NEG)
    send_st[...] = jnp.zeros_like(send_st)
    first = lax.broadcasted_iota(jnp.int32, (block, block), 0)
    second = lax.broadcasted_iota(jnp.int32, (block, block), 1)
    causal[...] = jnp.where(second <= first, 0.0, NEG)

    for g in range(kv_heads):
        cols = slice(g * HD, (g + 1) * HD)
        for index, target in ((0, kx), (1, vx)):
            target[g, 0:block] = kv_buf[index, :, cols]
            target[g, pl.ds(block, share)] = anchors[me, index, :, cols]
            target[g, pl.ds(near_keys, rows)] = qkv_buf[index, :, cols]
            rest = extra - near_keys - rows
            if rest:
                target[g, pl.ds(near_keys + rows, rest)] = jnp.zeros((rest, HD), jnp.bfloat16)

    def fold(block_scores):
        parts = [block_scores[:, k:k + HD] for k in range(0, block_scores.shape[1], HD)]
        return functools.reduce(jnp.maximum, parts)

    def less(block_scores, peak):
        if block_scores.shape[1] % HD:
            return block_scores - peak[:, 0:1]
        parts = [block_scores[:, k:k + HD] - peak for k in range(0, block_scores.shape[1], HD)]
        return jnp.concatenate(parts, axis=1)

    def stacked_queries(i):
        parts = []
        for j in range(STACK):
            at = pl.multiple_of((i * STACK + j) * HD, HD)
            parts.append(q_buf[:, pl.ds(at, HD)])
        return jnp.concatenate(parts, axis=0)

    steps = columns // HD // STACK

    def pipelined(first_step, count, begin, finish):
        begin(first_step, 0)

        def two_steps(k, carry):
            i = first_step + 2 * k
            begin(i + 1, 1)
            finish(i, 0)
            begin((i + 2) % steps, 0)
            finish(i + 1, 1)
            return carry

        lax.fori_loop(0, count // 2, two_steps, 0)

    def begin_near(i, slot):
        g = i * STACK // group
        part = scores(stacked_queries(i), kx[g, pl.ds(0, near_keys)])
        hidden = jnp.concatenate([causal[...]] * STACK, axis=0)
        part = jnp.concatenate([part[:, :block] + hidden, part[:, block:]], axis=1)
        s_near[slot][...] = part
        m_pair[slot][...] = jnp.broadcast_to(jnp.max(part, axis=1, keepdims=True), m_pair[slot].shape)

    def finish_near(i, slot):
        g = i * STACK // group
        m_blk[i] = m_pair[slot][...]
        weights = jnp.exp2(less(s_near[slot][...], m_pair[slot][...]))
        o_blk[i] = weighted(weights, with_ones(vx[g, pl.ds(0, near_keys)]))

    pipelined(0, steps, begin_near, finish_near)

    for g in range(kv_heads):
        pass_on(query_line(g))
    begin_line(anchor_line)

    length = len_ref[0]
    cache_load.wait()
    spare = kv_buf[0, 0:16, :][0:1]
    wide = cache_buf.shape[2]

    def trim(i, carry):
        at = pl.multiple_of(i * TRIM, TRIM)
        slot = lax.broadcasted_iota(jnp.int32, (TRIM, wide), 0) + at
        visible = jnp.where(slot < length, 1.0, 0.0).astype(jnp.bfloat16)
        keys = cache_buf[0, pl.ds(at, TRIM)]
        cache_buf[0, pl.ds(at, TRIM)] = keys * visible + spare * (1.0 - visible)
        cache_buf[1, pl.ds(at, TRIM)] = cache_buf[1, pl.ds(at, TRIM)] * visible
        ones[pl.ds(at, TRIM)] = visible[:, :HD]
        return carry

    lax.fori_loop(0, cache_count // TRIM, trim, 0)

    tiles = group // tile_heads
    items = [(g, t) for g in range(kv_heads) for t in range(tiles)]

    def open_item(k):
        g, t = items[k]
        s_buf, m_run, rows_in = s_bufs[k % 2], m_runs[k % 2], qg[k % 2]
        if t == 0:
            receive(query_line(g))
        for j in range(tile_heads):
            head = g * group + t * tile_heads + j
            rows_in[j * total:(j + 1) * total] = queries[:, head * HD:(head + 1) * HD]
        near = scores(rows_in[...], kx[g])
        tail = jnp.concatenate([xbias[...]] * tile_heads, axis=0)
        near_parts = [near[:, :near_keys], near[:, near_keys:near_keys + HD] + tail]
        if extra > near_keys + HD:
            near_parts.append(jnp.full((tile, extra - near_keys - HD), NEG, jnp.float32))
        near = jnp.concatenate(near_parts, axis=1)
        s_buf[:, cache_count:] = near
        m_run[...] = fold(near)

    def cached_scores(k, at):
        g = items[k][0]
        s_buf, m_run, rows_in = s_bufs[k % 2], m_runs[k % 2], qg[k % 2]
        part = scores(rows_in[...], cache_buf[0, pl.ds(at, CHUNK), g * HD:(g + 1) * HD])
        s_buf[:, pl.ds(at, CHUNK)] = part
        m_run[...] = jnp.maximum(m_run[...], fold(part))

    def near_values(k):
        g = items[k][0]
        s_buf, m_run = s_bufs[k % 2], m_runs[k % 2]
        peak = jnp.max(m_run[...], axis=1, keepdims=True)
        m_run[...] = jnp.broadcast_to(peak, m_run.shape)
        acc[...] = weighted(jnp.exp2(less(s_buf[:, cache_count:], m_run[...])), with_ones(vx[g]))

    def cached_values(k, at):
        g = items[k][0]
        s_buf, m_run = s_bufs[k % 2], m_runs[k % 2]
        weights = jnp.exp2(less(s_buf[:, pl.ds(at, CHUNK)], m_run[...]))
        values = jnp.concatenate(
            [cache_buf[1, pl.ds(at, CHUNK), g * HD:(g + 1) * HD], ones[pl.ds(at, CHUNK)]], axis=1)
        acc[...] += weighted(weights, values)

    def close_item(k):
        g, t = items[k]
        m_run = m_runs[k % 2]
        for j in range(tile_heads):
            head = g * group + t * tile_heads + j
            span = slice(j * total, (j + 1) * total)
            send_o[:, head * HD:(head + 1) * HD] = acc[span, :HD].astype(jnp.bfloat16)
            marked = jnp.where(lane == head, m_run[span], send_st[...])
            send_st[...] = jnp.where(lane == heads + head, acc[span, HD:], marked)
        if t == tiles - 1:
            for peer in peers:
                output_copy(g, me, peer).start()

    for k in range(len(items) + 1):
        if k < len(items):
            open_item(k)
        if k > 0:
            near_values(k - 1)

        def one_chunk(i, carry, k=k):
            at = pl.multiple_of(i * CHUNK, CHUNK)
            if k < len(items):
                cached_scores(k, at)
            if k > 0:
                cached_values(k - 1, at)
            return carry

        lax.fori_loop(0, cache_count // CHUNK, one_chunk, 0)
        if k > 0:
            close_item(k - 1)
        if k == min(1, len(items) - 1):
            pass_on(anchor_line)
    for peer in peers:
        stats_copy(me, peer).start()

    receive(anchor_line)
    for g in range(kv_heads):
        cols = slice(g * HD, (g + 1) * HD)
        for k, peer in enumerate(peers):
            kb[g, k * share:(k + 1) * share] = anchors[peer, 0, :, cols]
            vb[g, k * share:(k + 1) * share] = with_ones(anchors[peer, 1, :, cols])

    def begin_far(i, slot):
        part = scores(stacked_queries(i), kb[i * STACK // group])
        s_far[slot][...] = part
        m_pair[slot][...] = jnp.maximum(m_blk[i], jnp.max(part, axis=1, keepdims=True))

    def finish_far(i, slot):
        peak = m_pair[slot][...]
        result = weighted(jnp.exp2(less(s_far[slot][...], peak)), vb[i * STACK // group])
        factor = jnp.exp2(m_blk[i] - peak)
        top = result[:, :HD] + o_blk[i, :, :HD] * factor
        below = result[:, HD:] + o_blk[i, :, HD:] * factor
        final = (top / below).astype(jnp.bfloat16)
        for j in range(STACK):
            at = pl.multiple_of((i * STACK + j) * HD, HD)
            out_buf[:, pl.ds(at, HD)] = final[j * block:(j + 1) * block]

    pipelined(0, steps, begin_far, finish_far)
    for g in range(kv_heads):
        pltpu.make_async_copy(out_buf.at[:, half_of(g)], out_hbm.at[:, half_of(g)], out_sem.at[g]).start()

    for peer in peers:
        stats_copy(peer, peer).wait_recv()
        for g in range(kv_heads):
            output_copy(g, peer, peer).wait_recv()
    mine = rows_of(me)
    recv_st[me] = send_st[mine]
    recv_o[me] = send_o[mine]
    top = functools.reduce(jnp.maximum, [recv_st[c] for c in range(n)])
    factors = [jnp.exp2(recv_st[c] - top) for c in range(n)]
    totals = [pltpu.roll(recv_st[c], HD - heads, 1) for c in range(n)]
    whole = sum(factors[c] * totals[c] for c in range(n))
    for h in range(heads):
        span = slice(h * HD, (h + 1) * HD)
        merged = sum(
            recv_o[c, :, span].astype(jnp.float32) * factors[c][:, h:h + 1] for c in range(n)
        )
        qout_ref[:, span] = (merged / whole[:, h:h + 1]).astype(jnp.bfloat16)

    for g in range(kv_heads):
        pltpu.make_async_copy(out_buf.at[:, half_of(g)], out_hbm.at[:, half_of(g)], out_sem.at[g]).wait()
    drain(anchor_line)
    for g in range(kv_heads):
        drain(query_line(g))
    for peer in peers:
        stats_copy(me, peer).wait_send()
        for g in range(kv_heads):
            output_copy(g, me, peer).wait_send()


def hand_on(block_in, query_in, block_out, query_out, block_buf, query_buf, in_sems, out_sems):
    step = block_in.shape[0] // PIECES
    parts = [(query_in, query_buf, query_out)]
    for k in range(PIECES):
        span = pl.ds(k * step, step)
        parts.append((block_in.at[span], block_buf.at[span], block_out.at[span]))
    loads = [pltpu.make_async_copy(a, b, in_sems.at[k]) for k, (a, b, c) in enumerate(parts)]
    stores = [pltpu.make_async_copy(b, c, out_sems.at[k]) for k, (a, b, c) in enumerate(parts)]
    for load in loads:
        load.start()
    for load, store in zip(loads, stores):
        load.wait()
        store.start()
    for store in stores:
        store.wait()


def local(n, q_block, kv_block, anchor_kv, cache_kv, cache_len, query_q, query_kv, query_pos):
    own = query_q.shape[0]
    rows = -(-own // 16) * 16
    if rows != own:
        query_q = jnp.pad(query_q, ((0, rows - own), (0, 0)))
        query_kv = jnp.pad(query_kv, ((0, 0), (0, rows - own), (0, 0)))
    block, columns = q_block.shape
    kv_columns = kv_block.shape[2]
    kv_heads = kv_columns // HD
    group = columns // kv_columns
    share = anchor_kv.shape[1]
    cache_count = cache_kv.shape[1]
    total = n * rows
    tile = total * max(1, min(group, 512 // total))
    extra = -(-(block + share + HD) // HD) * HD
    far = (n - 1) * share
    bf16, f32 = jnp.bfloat16, jnp.float32
    vmem = pltpu.VMEM
    dma = pltpu.SemaphoreType.DMA
    hbm = pl.BlockSpec(memory_space=pl.ANY)
    stacked = STACK * block
    results = (
        jax.ShapeDtypeStruct((block, columns), bf16),
        jax.ShapeDtypeStruct((rows, columns), bf16),
    )
    block_out, query_out = pl.pallas_call(
        functools.partial(kernel, n, own),
        out_shape=results,
        in_specs=[hbm] * 8,
        out_specs=(hbm, pl.BlockSpec(memory_space=vmem)),
        scratch_shapes=[
            pltpu.SMEM(query_pos.shape, jnp.int32),
            pltpu.SMEM((1,), jnp.int32),
            vmem((block, columns), bf16),
            vmem((2, block, kv_columns), bf16),
            vmem((2, cache_count, kv_columns), bf16),
            vmem((2, rows, kv_columns), bf16),
            vmem((n, 2, share, kv_columns), bf16),
            vmem((total, columns), bf16),
            [vmem((tile, HD), bf16)] * 2,
            vmem((kv_heads, extra, HD), bf16),
            vmem((kv_heads, extra, HD), bf16),
            vmem((cache_count, HD), bf16),
            vmem((total, HD), f32),
            [vmem((tile, cache_count + extra), f32)] * 2,
            [vmem((tile, HD), f32)] * 2,
            vmem((tile, 2 * HD), f32),
            vmem((kv_heads, far, HD), bf16),
            vmem((kv_heads, far, 2 * HD), bf16),
            vmem((block, block), f32),
            [vmem((stacked, block + share), f32)] * 2,
            [vmem((stacked, far), f32)] * 2,
            [vmem((stacked, HD), f32)] * 2,
            vmem((columns // HD // STACK, STACK * block, HD), f32),
            vmem((columns // HD // STACK, STACK * block, 2 * HD), f32),
            vmem((block, columns), bf16),
            vmem((total, columns), bf16),
            vmem((total, HD), f32),
            vmem((n, rows, columns), bf16),
            vmem((n, rows, HD), f32),
            dma((8,)), dma((kv_heads,)),
            dma((kv_heads, 2, n)), dma((kv_heads, n)),
            dma((2, n)), dma((n,)),
            dma((kv_heads, n)), dma((kv_heads, n)),
            dma((n,)), dma((n,)),
        ],
        compiler_params=pltpu.CompilerParams(
            collective_id=0, has_side_effects=True, vmem_limit_bytes=56 * 1024 * 1024
        ),
    )(query_pos, cache_len, q_block, kv_block, anchor_kv, cache_kv, query_q, query_kv)
    block_out, query_out = pl.pallas_call(
        hand_on,
        out_shape=results,
        in_specs=[hbm, hbm],
        out_specs=(hbm, hbm),
        scratch_shapes=[
            vmem((block, columns), bf16), vmem((rows, columns), bf16), dma((PIECES + 1,)), dma((PIECES + 1,)),
        ],
    )(block_out, query_out)
    return block_out, query_out[:own]


def solution(mesh):
    in_specs = (
        P(("groups", "ctx"), "head"),
        P(None, ("groups", "ctx"), "head"),
        P(None, ("groups", "ctx"), "head"),
        P(None, ("groups", "ctx"), "head"),
        P(("groups", "ctx")),
        P(("groups", "ctx"), "head"),
        P(None, ("groups", "ctx"), "head"),
        P("groups"),
    )
    out_specs = (P(("groups", "ctx"), "head"), P(("groups", "ctx"), "head"))
    return jax.shard_map(
        functools.partial(local, mesh.shape["ctx"]),
        mesh=mesh, in_specs=in_specs, out_specs=out_specs, check_vma=False)
```

```python
import functools
import math

import jax
import jax.numpy as jnp
from jax import lax
from jax.experimental import pallas as pl
from jax.experimental.pallas import tpu as pltpu
from jax.sharding import PartitionSpec as P

HD = 128
NEG = -1e30
SCALE2 = math.log2(math.e) / math.sqrt(HD)
CHUNK = 2048
TRIM = 256
STACK = 2
PIECES = 4
MESH = pl.DeviceIdType.MESH


def scores(queries, keys):
    dims = (((1,), (1,)), ((), ()))
    return lax.dot_general(queries, keys, dims, preferred_element_type=jnp.float32) * SCALE2


def with_ones(values):
    return jnp.concatenate([values, jnp.ones_like(values)], axis=1)


def weighted(weights, values):
    return jnp.dot(weights.astype(jnp.bfloat16), values, preferred_element_type=jnp.float32)


def kernel(
    n, own,
    pos_hbm, len_hbm, q_hbm, kv_hbm, anchor_hbm, cache_hbm, qq_hbm, qkv_hbm,
    out_hbm, qout_ref,
    pos_ref, len_ref, q_buf, kv_buf, cache_buf, qkv_buf, anchors, queries,
    qg, kx, vx, ones, xbias, s_bufs, m_runs, acc, kb, vb, causal, s_near, s_far, m_pair, m_blk, o_blk, out_buf,
    send_o, send_st, recv_o, recv_st,
    in_sem, out_sem, q_send, q_recv, a_send, a_recv, o_send, o_recv, st_send, st_recv,
):
    me = lax.axis_index("ctx")
    peers = [lax.rem(me + k, n) for k in range(1, n)]
    rows = qq_hbm.shape[0]
    block = q_buf.shape[0]
    columns = q_buf.shape[1]
    kv_heads = kv_buf.shape[2] // HD
    group = columns // HD // kv_heads
    share = anchor_hbm.shape[1]
    cache_count = cache_buf.shape[1]
    total = n * rows
    extra = kx.shape[1]
    tile = acc.shape[0]
    tile_heads = tile // total
    half = group * HD
    heads = columns // HD
    near_keys = block + share

    def rows_of(who):
        return pl.ds(pl.multiple_of(who * rows, rows), rows)

    def half_of(g):
        return pl.ds(pl.multiple_of(g * half, half), half)

    loads = [
        pltpu.make_async_copy(qq_hbm, queries.at[rows_of(me)], in_sem.at[0]),
        pltpu.make_async_copy(anchor_hbm, anchors.at[me], in_sem.at[1]),
        pltpu.make_async_copy(kv_hbm, kv_buf, in_sem.at[2]),
        pltpu.make_async_copy(qkv_hbm, qkv_buf, in_sem.at[3]),
        pltpu.make_async_copy(q_hbm, q_buf, in_sem.at[4]),
        pltpu.make_async_copy(len_hbm, len_ref, in_sem.at[5]),
        pltpu.make_async_copy(pos_hbm, pos_ref, in_sem.at[7]),
    ]
    cache_load = pltpu.make_async_copy(cache_hbm, cache_buf, in_sem.at[6])
    for load in loads:
        load.start()
    cache_load.start()

    barrier = pltpu.get_barrier_semaphore()
    for peer in peers:
        pl.semaphore_signal(barrier, inc=1, device_id={"ctx": peer}, device_id_type=MESH)
    pl.semaphore_wait(barrier, n - 1)

    ways = (1, -1)
    reach = min(2, n - 1)

    def inside(host):
        return jnp.logical_and(host >= 0, host < n)

    def anchor_line(slot, target, sends, direct):
        return pltpu.make_async_remote_copy(
            src_ref=anchor_hbm if direct else anchors.at[slot], dst_ref=anchors.at[slot],
            send_sem=a_send.at[sends], recv_sem=a_recv.at[slot],
            device_id={"ctx": target}, device_id_type=MESH)

    def query_line(g):
        def line(slot, target, sends, direct):
            there = queries.at[rows_of(slot), half_of(g)]
            return pltpu.make_async_remote_copy(
                src_ref=qq_hbm.at[:, half_of(g)] if direct else there, dst_ref=there,
                send_sem=q_send.at[(g,) + sends], recv_sem=q_recv.at[g, slot],
                device_id={"ctx": target}, device_id_type=MESH)
        return line

    def sender(way, distance):
        return ((1 - way) // 2, distance - 1)

    def passed(line, way, distance):
        return line(me - way * (distance - 1), me + way, sender(way, distance), False)

    def for_each_direct(line, action):
        for distance in range(reach, 0, -1):
            for way in ways:
                @pl.when(inside(me + way * distance))
                def _():
                    action(line(me, me + way * distance, sender(way, distance), True))

    def for_each_passed(line, action):
        for distance in range(reach + 1, n):
            for way in ways:
                @pl.when(jnp.logical_and(inside(me - way * (distance - 1)), inside(me + way)))
                def _():
                    action(passed(line, way, distance))

    def begin_line(line):
        for_each_direct(line, lambda copy: copy.start())

    def pass_on(line):
        def receive_and_send(copy):
            copy.wait_recv()
            copy.start()
        for_each_passed(line, receive_and_send)

    def receive(line):
        for distance in range(1, n):
            for way in ways:
                here = inside(me - way * distance)
                if reach <= distance < n - 1:
                    here = jnp.logical_and(here, jnp.logical_not(inside(me + way)))

                @pl.when(here)
                def _():
                    passed(line, way, distance + 1).wait_recv()

    def drain(line):
        for_each_direct(line, lambda copy: copy.wait_send())
        for_each_passed(line, lambda copy: copy.wait_send())

    def output_copy(g, slot, peer):
        return pltpu.make_async_remote_copy(
            src_ref=send_o.at[rows_of(peer), half_of(g)],
            dst_ref=recv_o.at[slot, :, half_of(g)], send_sem=o_send.at[g, peer],
            recv_sem=o_recv.at[g, slot], device_id={"ctx": peer}, device_id_type=MESH)

    def stats_copy(slot, peer):
        return pltpu.make_async_remote_copy(
            src_ref=send_st.at[rows_of(peer)],
            dst_ref=recv_st.at[slot], send_sem=st_send.at[peer],
            recv_sem=st_recv.at[slot], device_id={"ctx": peer}, device_id_type=MESH)

    for g in range(kv_heads):
        begin_line(query_line(g))

    for load in loads:
        load.wait()

    row = lax.broadcasted_iota(jnp.int32, (total, HD), 0)
    lane = lax.broadcasted_iota(jnp.int32, (total, HD), 1)
    row_pos = jnp.zeros((total, HD), jnp.int32)
    for i in range(n * own):
        row_pos = jnp.where(row == (i // own) * rows + i % own, pos_ref[i], row_pos)
    key_pos = jnp.full((total, HD), 1 << 30, jnp.int32)
    for j in range(own):
        key_pos = jnp.where(lane == j, pos_ref[me * own + j], key_pos)
    xbias[...] = jnp.where(key_pos <= row_pos, 0.0, NEG)
    send_st[...] = jnp.zeros_like(send_st)
    first = lax.broadcasted_iota(jnp.int32, (block, block), 0)
    second = lax.broadcasted_iota(jnp.int32, (block, block), 1)
    causal[...] = jnp.where(second <= first, 0.0, NEG)

    for g in range(kv_heads):
        cols = slice(g * HD, (g + 1) * HD)
        for index, target in ((0, kx), (1, vx)):
            target[g, 0:block] = kv_buf[index, :, cols]
            target[g, pl.ds(block, share)] = anchors[me, index, :, cols]
            target[g, pl.ds(near_keys, rows)] = qkv_buf[index, :, cols]
            rest = extra - near_keys - rows
            if rest:
                target[g, pl.ds(near_keys + rows, rest)] = jnp.zeros((rest, HD), jnp.bfloat16)

    def fold(block_scores):
        parts = [block_scores[:, k:k + HD] for k in range(0, block_scores.shape[1], HD)]
        return functools.reduce(jnp.maximum, parts)

    def less(block_scores, peak):
        if block_scores.shape[1] % HD:
            return block_scores - peak[:, 0:1]
        parts = [block_scores[:, k:k + HD] - peak for k in range(0, block_scores.shape[1], HD)]
        return jnp.concatenate(parts, axis=1)

    def stacked_queries(i):
        parts = []
        for j in range(STACK):
            at = pl.multiple_of((i * STACK + j) * HD, HD)
            parts.append(q_buf[:, pl.ds(at, HD)])
        return jnp.concatenate(parts, axis=0)

    steps = columns // HD // STACK

    def pipelined(first_step, count, begin, finish):
        begin(first_step, 0)

        def two_steps(k, carry):
            i = first_step + 2 * k
            begin(i + 1, 1)
            finish(i, 0)
            begin((i + 2) % steps, 0)
            finish(i + 1, 1)
            return carry

        lax.fori_loop(0, count // 2, two_steps, 0)

    def begin_near(i, slot):
        g = i * STACK // group
        part = scores(stacked_queries(i), kx[g, pl.ds(0, near_keys)])
        hidden = jnp.concatenate([causal[...]] * STACK, axis=0)
        part = jnp.concatenate([part[:, :block] + hidden, part[:, block:]], axis=1)
        s_near[slot][...] = part
        m_pair[slot][...] = jnp.broadcast_to(jnp.max(part, axis=1, keepdims=True), m_pair[slot].shape)

    def finish_near(i, slot):
        g = i * STACK // group
        m_blk[i] = m_pair[slot][...]
        weights = jnp.exp2(less(s_near[slot][...], m_pair[slot][...]))
        o_blk[i] = weighted(weights, with_ones(vx[g, pl.ds(0, near_keys)]))

    pipelined(0, steps, begin_near, finish_near)


    length = len_ref[0]
    cache_load.wait()
    spare = kv_buf[0, 0:16, :][0:1]
    wide = cache_buf.shape[2]

    def trim(i, carry):
        at = pl.multiple_of(i * TRIM, TRIM)
        slot = lax.broadcasted_iota(jnp.int32, (TRIM, wide), 0) + at
        visible = jnp.where(slot < length, 1.0, 0.0).astype(jnp.bfloat16)
        keys = cache_buf[0, pl.ds(at, TRIM)]
        cache_buf[0, pl.ds(at, TRIM)] = keys * visible + spare * (1.0 - visible)
        cache_buf[1, pl.ds(at, TRIM)] = cache_buf[1, pl.ds(at, TRIM)] * visible
        ones[pl.ds(at, TRIM)] = visible[:, :HD]
        return carry

    lax.fori_loop(0, cache_count // TRIM, trim, 0)

    for g in range(kv_heads):
        pass_on(query_line(g))
    begin_line(anchor_line)

    tiles = group // tile_heads
    items = [(g, t) for g in range(kv_heads) for t in range(tiles)]

    def open_item(k):
        g, t = items[k]
        s_buf, m_run, rows_in = s_bufs[k % 2], m_runs[k % 2], qg[k % 2]
        if t == 0:
            receive(query_line(g))
        for j in range(tile_heads):
            head = g * group + t * tile_heads + j
            rows_in[j * total:(j + 1) * total] = queries[:, head * HD:(head + 1) * HD]
        near = scores(rows_in[...], kx[g])
        tail = jnp.concatenate([xbias[...]] * tile_heads, axis=0)
        near_parts = [near[:, :near_keys], near[:, near_keys:near_keys + HD] + tail]
        if extra > near_keys + HD:
            near_parts.append(jnp.full((tile, extra - near_keys - HD), NEG, jnp.float32))
        near = jnp.concatenate(near_parts, axis=1)
        s_buf[:, cache_count:] = near
        m_run[...] = fold(near)

    def cached_scores(k, at):
        g = items[k][0]
        s_buf, m_run, rows_in = s_bufs[k % 2], m_runs[k % 2], qg[k % 2]
        part = scores(rows_in[...], cache_buf[0, pl.ds(at, CHUNK), g * HD:(g + 1) * HD])
        s_buf[:, pl.ds(at, CHUNK)] = part
        m_run[...] = jnp.maximum(m_run[...], fold(part))

    def near_values(k):
        g = items[k][0]
        s_buf, m_run = s_bufs[k % 2], m_runs[k % 2]
        peak = jnp.max(m_run[...], axis=1, keepdims=True)
        m_run[...] = jnp.broadcast_to(peak, m_run.shape)
        acc[...] = weighted(jnp.exp2(less(s_buf[:, cache_count:], m_run[...])), with_ones(vx[g]))

    def cached_values(k, at):
        g = items[k][0]
        s_buf, m_run = s_bufs[k % 2], m_runs[k % 2]
        weights = jnp.exp2(less(s_buf[:, pl.ds(at, CHUNK)], m_run[...]))
        values = jnp.concatenate(
            [cache_buf[1, pl.ds(at, CHUNK), g * HD:(g + 1) * HD], ones[pl.ds(at, CHUNK)]], axis=1)
        acc[...] += weighted(weights, values)

    def close_item(k):
        g, t = items[k]
        m_run = m_runs[k % 2]
        for j in range(tile_heads):
            head = g * group + t * tile_heads + j
            span = slice(j * total, (j + 1) * total)
            send_o[:, head * HD:(head + 1) * HD] = acc[span, :HD].astype(jnp.bfloat16)
            marked = jnp.where(lane == head, m_run[span], send_st[...])
            send_st[...] = jnp.where(lane == heads + head, acc[span, HD:], marked)
        if t == tiles - 1:
            for peer in peers:
                output_copy(g, me, peer).start()

    for k in range(len(items) + 1):
        if k < len(items):
            open_item(k)
        if k > 0:
            near_values(k - 1)

        def one_chunk(i, carry, k=k):
            at = pl.multiple_of(i * CHUNK, CHUNK)
            if k < len(items):
                cached_scores(k, at)
            if k > 0:
                cached_values(k - 1, at)
            return carry

        lax.fori_loop(0, cache_count // CHUNK, one_chunk, 0)
        if k > 0:
            close_item(k - 1)
        if k == min(1, len(items) - 1):
            pass_on(anchor_line)
    for peer in peers:
        stats_copy(me, peer).start()

    receive(anchor_line)
    for g in range(kv_heads):
        cols = slice(g * HD, (g + 1) * HD)
        for k, peer in enumerate(peers):
            kb[g, k * share:(k + 1) * share] = anchors[peer, 0, :, cols]
            vb[g, k * share:(k + 1) * share] = with_ones(anchors[peer, 1, :, cols])

    def begin_far(i, slot):
        part = scores(stacked_queries(i), kb[i * STACK // group])
        s_far[slot][...] = part
        m_pair[slot][...] = jnp.maximum(m_blk[i], jnp.max(part, axis=1, keepdims=True))

    def finish_far(i, slot):
        peak = m_pair[slot][...]
        result = weighted(jnp.exp2(less(s_far[slot][...], peak)), vb[i * STACK // group])
        factor = jnp.exp2(m_blk[i] - peak)
        top = result[:, :HD] + o_blk[i, :, :HD] * factor
        below = result[:, HD:] + o_blk[i, :, HD:] * factor
        final = (top / below).astype(jnp.bfloat16)
        for j in range(STACK):
            at = pl.multiple_of((i * STACK + j) * HD, HD)
            out_buf[:, pl.ds(at, HD)] = final[j * block:(j + 1) * block]

    pipelined(0, steps, begin_far, finish_far)
    for g in range(kv_heads):
        pltpu.make_async_copy(out_buf.at[:, half_of(g)], out_hbm.at[:, half_of(g)], out_sem.at[g]).start()

    for peer in peers:
        stats_copy(peer, peer).wait_recv()
        for g in range(kv_heads):
            output_copy(g, peer, peer).wait_recv()
    mine = rows_of(me)
    recv_st[me] = send_st[mine]
    recv_o[me] = send_o[mine]
    top = functools.reduce(jnp.maximum, [recv_st[c] for c in range(n)])
    factors = [jnp.exp2(recv_st[c] - top) for c in range(n)]
    totals = [pltpu.roll(recv_st[c], HD - heads, 1) for c in range(n)]
    whole = sum(factors[c] * totals[c] for c in range(n))
    for h in range(heads):
        span = slice(h * HD, (h + 1) * HD)
        merged = sum(
            recv_o[c, :, span].astype(jnp.float32) * factors[c][:, h:h + 1] for c in range(n)
        )
        qout_ref[:, span] = (merged / whole[:, h:h + 1]).astype(jnp.bfloat16)

    for g in range(kv_heads):
        pltpu.make_async_copy(out_buf.at[:, half_of(g)], out_hbm.at[:, half_of(g)], out_sem.at[g]).wait()
    drain(anchor_line)
    for g in range(kv_heads):
        drain(query_line(g))
    for peer in peers:
        stats_copy(me, peer).wait_send()
        for g in range(kv_heads):
            output_copy(g, me, peer).wait_send()


def hand_on(block_in, query_in, block_out, query_out, block_buf, query_buf, in_sems, out_sems):
    step = block_in.shape[0] // PIECES
    parts = [(query_in, query_buf, query_out)]
    for k in range(PIECES):
        span = pl.ds(k * step, step)
        parts.append((block_in.at[span], block_buf.at[span], block_out.at[span]))
    loads = [pltpu.make_async_copy(a, b, in_sems.at[k]) for k, (a, b, c) in enumerate(parts)]
    stores = [pltpu.make_async_copy(b, c, out_sems.at[k]) for k, (a, b, c) in enumerate(parts)]
    for load in loads:
        load.start()
    for load, store in zip(loads, stores):
        load.wait()
        store.start()
    for store in stores:
        store.wait()


def local(n, q_block, kv_block, anchor_kv, cache_kv, cache_len, query_q, query_kv, query_pos):
    own = query_q.shape[0]
    rows = -(-own // 16) * 16
    if rows != own:
        query_q = jnp.pad(query_q, ((0, rows - own), (0, 0)))
        query_kv = jnp.pad(query_kv, ((0, 0), (0, rows - own), (0, 0)))
    block, columns = q_block.shape
    kv_columns = kv_block.shape[2]
    kv_heads = kv_columns // HD
    group = columns // kv_columns
    share = anchor_kv.shape[1]
    cache_count = cache_kv.shape[1]
    total = n * rows
    tile = total * max(1, min(group, 512 // total))
    extra = -(-(block + share + HD) // HD) * HD
    far = (n - 1) * share
    bf16, f32 = jnp.bfloat16, jnp.float32
    vmem = pltpu.VMEM
    dma = pltpu.SemaphoreType.DMA
    hbm = pl.BlockSpec(memory_space=pl.ANY)
    stacked = STACK * block
    results = (
        jax.ShapeDtypeStruct((block, columns), bf16),
        jax.ShapeDtypeStruct((rows, columns), bf16),
    )
    block_out, query_out = pl.pallas_call(
        functools.partial(kernel, n, own),
        out_shape=results,
        in_specs=[hbm] * 8,
        out_specs=(hbm, pl.BlockSpec(memory_space=vmem)),
        scratch_shapes=[
            pltpu.SMEM(query_pos.shape, jnp.int32),
            pltpu.SMEM((1,), jnp.int32),
            vmem((block, columns), bf16),
            vmem((2, block, kv_columns), bf16),
            vmem((2, cache_count, kv_columns), bf16),
            vmem((2, rows, kv_columns), bf16),
            vmem((n, 2, share, kv_columns), bf16),
            vmem((total, columns), bf16),
            [vmem((tile, HD), bf16)] * 2,
            vmem((kv_heads, extra, HD), bf16),
            vmem((kv_heads, extra, HD), bf16),
            vmem((cache_count, HD), bf16),
            vmem((total, HD), f32),
            [vmem((tile, cache_count + extra), f32)] * 2,
            [vmem((tile, HD), f32)] * 2,
            vmem((tile, 2 * HD), f32),
            vmem((kv_heads, far, HD), bf16),
            vmem((kv_heads, far, 2 * HD), bf16),
            vmem((block, block), f32),
            [vmem((stacked, block + share), f32)] * 2,
            [vmem((stacked, far), f32)] * 2,
            [vmem((stacked, HD), f32)] * 2,
            vmem((columns // HD // STACK, STACK * block, HD), f32),
            vmem((columns // HD // STACK, STACK * block, 2 * HD), f32),
            vmem((block, columns), bf16),
            vmem((total, columns), bf16),
            vmem((total, HD), f32),
            vmem((n, rows, columns), bf16),
            vmem((n, rows, HD), f32),
            dma((8,)), dma((kv_heads,)),
            dma((kv_heads, 2, n)), dma((kv_heads, n)),
            dma((2, n)), dma((n,)),
            dma((kv_heads, n)), dma((kv_heads, n)),
            dma((n,)), dma((n,)),
        ],
        compiler_params=pltpu.CompilerParams(
            collective_id=0, has_side_effects=True, vmem_limit_bytes=56 * 1024 * 1024
        ),
    )(query_pos, cache_len, q_block, kv_block, anchor_kv, cache_kv, query_q, query_kv)
    block_out, query_out = pl.pallas_call(
        hand_on,
        out_shape=results,
        in_specs=[hbm, hbm],
        out_specs=(hbm, hbm),
        scratch_shapes=[
            vmem((block, columns), bf16), vmem((rows, columns), bf16), dma((PIECES + 1,)), dma((PIECES + 1,)),
        ],
    )(block_out, query_out)
    return block_out, query_out[:own]


def solution(mesh):
    in_specs = (
        P(("groups", "ctx"), "head"),
        P(None, ("groups", "ctx"), "head"),
        P(None, ("groups", "ctx"), "head"),
        P(None, ("groups", "ctx"), "head"),
        P(("groups", "ctx")),
        P(("groups", "ctx"), "head"),
        P(None, ("groups", "ctx"), "head"),
        P("groups"),
    )
    out_specs = (P(("groups", "ctx"), "head"), P(("groups", "ctx"), "head"))
    return jax.shard_map(
        functools.partial(local, mesh.shape["ctx"]),
        mesh=mesh, in_specs=in_specs, out_specs=out_specs, check_vma=False)
```
